32 devices in a mesh: item: 8 (over y, x, core), code: 4 (over z).
Axes of the slice: x: 2, y: 2, z: 4, core: 2. Of those that a mesh axis runs over, the one named last changes fastest.
Arguments:
- embeddings: bfloat16 [512, 65536], P('code', 'item'), may hold values from -6 to 6
- first_codes: int32 [65536], P('item'), may hold values from 0 to 8191
- second_codes: int32 [65536], P('item'), may hold values from 0 to 8191
- first_old: float32 [512, 8192], P('code', 'item'), may hold values from -6 to 6
- second_old: float32 [512, 8192], P('code', 'item'), may hold values from -3 to 3
Outputs:
- first_new: float32 [512, 8192], P('code', 'item')
- second_new: float32 [512, 8192], P('code', 'item')
- leftover: float32 [512, 65536], P('code', 'item')
The draws below stay inside these ranges and needn't reach their ends.
All inputs are finite; a program needn't handle non-finite values.
Results may differ from the reference program's by a relative error of at most 0.0003.
Values sent between devices are 32-bit elements; how exact they have to be, the bound alone decides.
A program may use at most 64 MiB of HBM per device.

```python
import jax
import jax.numpy as jnp
from jax import lax

D = 512
K = 8192
ITEMS = 65536


def plant(values, rng, low, largest):
    index_at = [jax.random.randint(jax.random.fold_in(rng, axis), (), 0, length) for axis, length in enumerate(values.shape)]
    widest = values.shape.index(max(values.shape))
    neighbour = index_at[:widest] + [(index_at[widest] + 1) % values.shape[widest]] + index_at[widest + 1:]
    return values.at[tuple(index_at)].set(low).at[tuple(neighbour)].set(largest)


def levels(rng, shape, cuts, low, high):
    level, own = 1.0, jax.random.fold_in(rng, 6)
    for axis_at, blocks in cuts:
        draws = jnp.exp(jax.random.uniform(jax.random.fold_in(own, axis_at), (blocks,), jnp.float32, low / len(cuts), high / len(cuts)))
        level = level * jnp.repeat(draws, shape[axis_at] // blocks).reshape([-1 if axis == axis_at else 1 for axis in range(len(shape))])
    return level


def bell_draw(rng, extent, deviation, reach, split=(), held_as=jnp.bfloat16):
    values = deviation * jax.random.normal(rng, extent, jnp.float32)
    if split:
        values = values * levels(rng, extent, split, -0.22, 0.18)
    return jnp.clip(values, -reach, reach).astype(held_as)


def setup_inputs(seed: int = 0) -> dict:
    arg_keys = jax.random.split(jax.random.key(seed), 6)
    embeddings = bell_draw(arg_keys[0], (D, ITEMS), 1.0, 6.0, ((0, 4), (1, 8)))
    first_codes = plant(jax.random.randint(arg_keys[1], (ITEMS,), 0, K), jax.random.fold_in(arg_keys[1], 1), 0, K - 1).astype(jnp.int32)
    second_codes = plant(jax.random.randint(arg_keys[2], (ITEMS,), 0, K), jax.random.fold_in(arg_keys[2], 1), 0, K - 1).astype(jnp.int32)
    first_old = bell_draw(arg_keys[3], (D, K), 1.0, 6.0, ((0, 4), (1, 8)), jnp.float32)
    second_old = bell_draw(arg_keys[4], (D, K), 0.5, 3.0, ((0, 4), (1, 8)), jnp.float32)
    return {"embeddings": embeddings, "first_codes": first_codes, "second_codes": second_codes, "first_old": first_old, "second_old": second_old}


def update(columns, codes, old):
    sums = jax.ops.segment_sum(columns.T, codes, num_segments=K).T
    counts = jax.ops.segment_sum(jnp.ones(codes.shape, jnp.float32), codes, num_segments=K)
    return 0.5 * old + 0.5 * sums / (counts + 1.0)[None, :]

def reference(embeddings, first_codes, second_codes, first_old, second_old):
    values = embeddings.astype(jnp.float32)
    normed = values * jax.lax.rsqrt(lax.optimization_barrier(jnp.mean(values * values, axis=0, keepdims=True)) + 1e-06)
    first_new = update(normed, first_codes, first_old)
    middle = normed - jnp.take(first_new, first_codes, axis=1)
    second_new = update(middle, second_codes, second_old)
    leftover = middle - jnp.take(second_new, second_codes, axis=1)
    return (first_new, second_new, leftover)
```

```python
import functools
import itertools

import jax
import jax.numpy as jnp
from jax import lax
from jax.experimental import pallas as pl
from jax.experimental.pallas import tpu as pltpu
from jax.sharding import PartitionSpec as P

D = 512
LANES = 128
GROUP = 8
PILES = 4
VMEM_BYTES = 52 * 1024 * 1024

VMEM = pl.BlockSpec(memory_space=pltpu.VMEM)
SMEM = pl.BlockSpec(memory_space=pltpu.SMEM)


def flip(me, bits):
    other = me
    for bit in bits:
        weight = 2**bit
        other = other + weight - 2 * weight * lax.rem(lax.div(me, weight), 2)
    return other


def subsets(bits, choice):
    return [tuple(b for b, c in zip(bits, pick) if c) for pick in itertools.product(choice, repeat=len(bits))]


def scales_kernel(n, e_ref, scale_ref, parts, send_sems, recv_sems):
    me = lax.axis_index("code")
    barrier = pltpu.get_barrier_semaphore()
    for step in range(1, n):
        pl.semaphore_signal(barrier, inc=1, device_id={"code": lax.rem(me + step, n)}, device_id_type=pl.DeviceIdType.MESH)
    items = e_ref.shape[1]
    width = min(items, 8 * LANES)

    @pl.loop(0, items // width)
    def _(at):
        columns = pl.ds(pl.multiple_of(at * width, width), width)
        values = e_ref[:, columns].astype(jnp.float32)
        parts[0, :, columns] = jnp.sum(values * values, axis=0, keepdims=True)

    pl.semaphore_wait(barrier, n - 1)
    copies = []
    for step in range(1, n):
        copy = pltpu.make_async_remote_copy(
            src_ref=parts.at[0],
            dst_ref=parts.at[step],
            send_sem=send_sems.at[step],
            recv_sem=recv_sems.at[step],
            device_id={"code": lax.rem(me + step, n)},
            device_id_type=pl.DeviceIdType.MESH,
        )
        copy.start()
        copies.append(copy)
    for copy in copies:
        copy.wait()
    squares = parts[0]
    for step in range(1, n):
        squares = squares + parts[step]
    scale_ref[...] = lax.rsqrt(squares / D + 1e-06)


def scales_of(embeddings, n):
    items = embeddings.shape[1]
    return pl.pallas_call(
        functools.partial(scales_kernel, n),
        out_shape=jax.ShapeDtypeStruct((1, items), jnp.float32),
        in_specs=[VMEM],
        out_specs=VMEM,
        scratch_shapes=[
            pltpu.VMEM((n, 1, items), jnp.float32),
            pltpu.SemaphoreType.DMA((n,)),
            pltpu.SemaphoreType.DMA((n,)),
        ],
        compiler_params=pltpu.CompilerParams(collective_id=0, has_side_effects=True, vmem_limit_bytes=VMEM_BYTES),
        cost_estimate=pl.CostEstimate(flops=0, bytes_accessed=16 * 2**20, transcendentals=0),
        name="scales",
    )(embeddings)


def clear(piles):
    rows = piles[0].shape[0]
    step = min(rows, 256)

    @pl.loop(0, rows // step)
    def _(at):
        for pile in piles:
            pile[pl.ds(pl.multiple_of(at * step, step), step), :] = jnp.zeros((step, pile.shape[1]), pile.dtype)


def merge(piles):
    rows = piles[0].shape[0]
    step = min(rows, 256)

    @pl.loop(0, rows // step)
    def _(at):
        where = pl.ds(pl.multiple_of(at * step, step), step)
        piles[0][where, :] = (piles[0][where, :] + piles[1][where, :]) + (piles[2][where, :] + piles[3][where, :])


def add_rows(piles, codes, rows):
    held = [piles[at % PILES][pl.ds(code, 1), :] for at, code in enumerate(codes)]
    first = [held[at] + rows[at] for at in range(PILES)]
    second = [
        jnp.where(codes[at] == codes[at + PILES], first[at], held[at + PILES]) + rows[at + PILES] for at in range(PILES)
    ]
    for at in range(PILES):
        piles[at][pl.ds(codes[at], 1), :] = first[at]
    for at in range(PILES):
        piles[at][pl.ds(codes[at + PILES], 1), :] = second[at]


def first_kernel(codes_ref, e_ref, scale_ref, normed_ref, sums_ref, *more):
    piles = (sums_ref,) + more
    items = e_ref.shape[1]
    clear(piles)

    @pl.loop(0, items // LANES)
    def _(at):
        span = pl.ds(pl.multiple_of(at * LANES, LANES), LANES)
        normed_ref[span, :] = (e_ref[:, span].astype(jnp.float32) * scale_ref[:, span]).T

    @pl.loop(0, items // GROUP, unroll=2)
    def _(at):
        base = pl.multiple_of(at * GROUP, GROUP)
        rows = [normed_ref[pl.ds(base + j, 1), :] for j in range(GROUP)]
        add_rows(piles, [codes_ref[base + j] for j in range(GROUP)], rows)

    merge(piles)


def second_kernel(first_ref, second_ref, normed_ref, table_ref, middle_ref, sums_ref, *more):
    piles = (sums_ref,) + more
    items = normed_ref.shape[0]
    clear(piles)

    @pl.loop(0, items // GROUP, unroll=2)
    def _(at):
        base = pl.multiple_of(at * GROUP, GROUP)
        rows = [
            normed_ref[pl.ds(base + j, 1), :] - table_ref[pl.ds(first_ref[base + j], 1), :] for j in range(GROUP)
        ]
        add_rows(piles, [second_ref[base + j] for j in range(GROUP)], rows)
        for j in range(GROUP):
            middle_ref[pl.ds(base + j, 1), :] = rows[j]

    merge(piles)


def last_kernel(block, codes_ref, middle_ref, table_ref, out_ref, named):
    start = pl.program_id(0) * block

    @pl.loop(0, block // GROUP, unroll=2)
    def _(at):
        base = pl.multiple_of(at * GROUP, GROUP)
        rows = [table_ref[pl.ds(codes_ref[start + base + j], 1), :] for j in range(GROUP)]
        for j in range(GROUP):
            named[pl.ds(base + j, 1), :] = rows[j]

    @pl.loop(0, block // LANES)
    def _(at):
        span = pl.ds(pl.multiple_of(at * LANES, LANES), LANES)
        out_ref[:, span] = (middle_ref[span, :] - named[span, :]).T


def exchange_kernel(n, sums_ref, old_ref, inverse_ref, whole_ref, own_ref, slots, send_in, recv_in, send_out, recv_out):
    levels = n.bit_length() - 1
    me = lax.axis_index("item")
    size = sums_ref.shape[0] // n
    half = size // 2
    rest = list(range(1, levels))
    orders = ([0] + rest, [0] + rest[::-1])

    def block(owner, path):
        return pl.ds(pl.multiple_of(owner * size + path * half, half), half)

    place_in, place_out = {}, {}
    for path, order in enumerate(orders):
        for step in range(levels):
            for far in subsets(order[step + 1:], (1, 0)):
                place_in[path, step, frozenset(far)] = len(place_in)
            for held in subsets(order[::-1][:step], (0, 1)):
                place_out[path, step, frozenset(held)] = len(place_out)

    sent = []

    def send_sum(path, step, far, source):
        slot = place_in[path, step, frozenset(far)]
        copy = pltpu.make_async_remote_copy(
            src_ref=source,
            dst_ref=slots.at[slot],
            send_sem=send_in.at[slot],
            recv_sem=recv_in.at[slot],
            device_id={"item": flip(me, [orders[path][step]])},
            device_id_type=pl.DeviceIdType.MESH,
        )
        copy.start()
        sent.append(copy)

    def new_copy(path, step, held, rows):
        slot = place_out[path, step, frozenset(held)]
        return pltpu.make_async_remote_copy(
            src_ref=whole_ref.at[rows],
            dst_ref=whole_ref.at[rows],
            send_sem=send_out.at[slot],
            recv_sem=recv_out.at[slot],
            device_id={"item": flip(me, [orders[path][::-1][step]])},
            device_id_type=pl.DeviceIdType.MESH,
        )

    def send_new(path, step, held):
        copy = new_copy(path, step, held, block(flip(me, held), path))
        copy.start()
        sent.append(copy)

    barrier = pltpu.get_barrier_semaphore()
    for bit in range(levels):
        pl.semaphore_signal(barrier, inc=1, device_id={"item": flip(me, [bit])}, device_id_type=pl.DeviceIdType.MESH)
    pl.semaphore_wait(barrier, levels)

    for fars in zip(*(subsets(order[1:], (1, 0)) for order in orders)):
        for path, far in enumerate(fars):
            send_sum(path, 0, far, sums_ref.at[block(flip(me, (0,) + far), path)])
    for step in range(levels):
        for fars in zip(*(subsets(order[step + 1:], (1, 0)) for order in orders)):
            for path, far in enumerate(fars):
                slot = place_in[path, step, frozenset(far)]
                pltpu.make_async_remote_copy(
                    src_ref=slots.at[slot],
                    dst_ref=slots.at[slot],
                    send_sem=send_in.at[slot],
                    recv_sem=recv_in.at[slot],
                    device_id={"item": flip(me, [orders[path][step]])},
                    device_id_type=pl.DeviceIdType.MESH,
                ).wait_recv()
                if step == 0:
                    mine = sums_ref[block(flip(me, far), path), :]
                else:
                    mine = slots[place_in[path, step - 1, frozenset(far)]]
                total = slots[slot] + mine
                if step < levels - 1:
                    slots[slot] = total
                    ahead = orders[path][step + 1]
                    if ahead in far:
                        send_sum(path, step + 1, tuple(b for b in far if b != ahead), slots.at[slot])
                else:
                    rows = pl.ds(path * half, half)
                    new = old_ref[rows, :] + total * inverse_ref[rows, :]
                    own_ref[rows, :] = new
                    whole_ref[block(me, path), :] = new
                    for later in range(levels):
                        send_new(path, later, ())

    for step in range(levels):
        for helds in zip(*(subsets(order[::-1][:step], (0, 1)) for order in orders)):
            for path, held in enumerate(helds):
                got = held + (orders[path][::-1][step],)
                new_copy(path, step, held, block(flip(me, got), path)).wait_recv()
                for later in range(step + 1, levels):
                    send_new(path, later, got)
    for copy in sent:
        copy.wait_send()


def exchange(sums, old, inverse, n, collective_id):
    rows, width = sums.shape
    size = rows // n
    count = 2 * (n - 1)
    return pl.pallas_call(
        functools.partial(exchange_kernel, n),
        out_shape=(jax.ShapeDtypeStruct(sums.shape, jnp.float32), jax.ShapeDtypeStruct((size, width), jnp.float32)),
        in_specs=[VMEM] * 3,
        out_specs=(VMEM, VMEM),
        scratch_shapes=[
            pltpu.VMEM((count, size // 2, width), jnp.float32),
            pltpu.SemaphoreType.DMA((count,)),
            pltpu.SemaphoreType.DMA((count,)),
            pltpu.SemaphoreType.DMA((count,)),
            pltpu.SemaphoreType.DMA((count,)),
        ],
        compiler_params=pltpu.CompilerParams(
            collective_id=collective_id, has_side_effects=True, vmem_limit_bytes=VMEM_BYTES
        ),
        cost_estimate=pl.CostEstimate(flops=0, bytes_accessed=128 * 2**20, transcendentals=0),
        name="exchange",
    )(sums, old, inverse)


def counts_of(codes, total):
    high = lax.shift_right_logical(codes, 7)[None, :] == jnp.arange(total // LANES, dtype=codes.dtype)[:, None]
    low = lax.bitwise_and(codes, LANES - 1)[None, :] == jnp.arange(LANES, dtype=codes.dtype)[:, None]
    return lax.dot_general(
        high.astype(jnp.bfloat16),
        low.astype(jnp.bfloat16),
        (((1,), (1,)), ((), ())),
        preferred_element_type=jnp.float32,
    )


def on_device(owners, feature_parts, embeddings, first_codes, second_codes, first_old, second_old):
    width, items = embeddings.shape
    total = first_old.shape[1] * owners
    f32 = jnp.float32
    local = pltpu.CompilerParams(vmem_limit_bytes=VMEM_BYTES)
    cost = pl.CostEstimate(flops=0, bytes_accessed=64 * 2**20, transcendentals=0)

    counts = jnp.stack([counts_of(first_codes, total), counts_of(second_codes, total)], axis=1)
    counts = lax.psum_scatter(counts, "item", scatter_dimension=0, tiled=True)
    halves = 0.5 / (counts + 1.0)
    first_inverse, second_inverse = (
        jnp.broadcast_to(halves[:, level].reshape(-1, 1), (total // owners, width)) for level in range(2)
    )
    piles = [pltpu.VMEM((total, width), f32)] * (PILES - 1)
    row_sums = jax.ShapeDtypeStruct((total, width), f32)
    row_items = jax.ShapeDtypeStruct((items, width), f32)

    scales = scales_of(embeddings, feature_parts)
    normed, first_sums = pl.pallas_call(
        first_kernel,
        out_shape=(row_items, row_sums),
        in_specs=[SMEM, VMEM, VMEM],
        out_specs=(VMEM, VMEM),
        scratch_shapes=piles,
        compiler_params=local,
        cost_estimate=cost,
        name="first_sums",
    )(first_codes, embeddings, scales)
    first_whole, first_own = exchange(first_sums, 0.5 * first_old.T, first_inverse, owners, 1)
    middle, second_sums = pl.pallas_call(
        second_kernel,
        out_shape=(row_items, row_sums),
        in_specs=[SMEM, SMEM, VMEM, VMEM],
        out_specs=(VMEM, VMEM),
        scratch_shapes=piles,
        compiler_params=local,
        cost_estimate=cost,
        name="second_sums",
    )(first_codes, second_codes, normed, first_whole)
    second_whole, second_own = exchange(second_sums, 0.5 * second_old.T, second_inverse, owners, 2)
    block = min(items, 1024)
    leftover = pl.pallas_call(
        functools.partial(last_kernel, block),
        out_shape=jax.ShapeDtypeStruct((width, items), f32),
        grid=(items // block,),
        in_specs=[
            SMEM,
            pl.BlockSpec((block, width), lambda at: (at, 0)),
            pl.BlockSpec((total, width), lambda at: (0, 0)),
        ],
        out_specs=pl.BlockSpec((width, block), lambda at: (0, at)),
        scratch_shapes=[pltpu.VMEM((block, width), f32)],
        compiler_params=local,
        cost_estimate=cost,
        name="leftover",
    )(second_codes, middle, second_whole)
    return (first_own.T, second_own.T, leftover)


def solution(mesh):
    in_specs = (P("code", "item"), P("item"), P("item"), P("code", "item"), P("code", "item"))
    out_specs = (P("code", "item"), P("code", "item"), P("code", "item"))
    return jax.shard_map(
        functools.partial(on_device, mesh.shape["item"], mesh.shape["code"]),
        mesh=mesh,
        in_specs=in_specs,
        out_specs=out_specs,
        check_vma=False,
    )
```

```python
import functools
import itertools

import jax
import jax.numpy as jnp
from jax import lax
from jax.experimental import pallas as pl
from jax.experimental.pallas import tpu as pltpu
from jax.sharding import PartitionSpec as P

D = 512
LANES = 128
PILES = 8
GROUP = 2 * PILES
SPAN = 64
MIB = 2**20

VMEM = pl.BlockSpec(memory_space=pltpu.VMEM)
SMEM = pl.BlockSpec(memory_space=pltpu.SMEM)


def flip(me, bits):
    other = me
    for bit in bits:
        weight = 2**bit
        other = other + weight - 2 * weight * lax.rem(lax.div(me, weight), 2)
    return other


def subsets(bits, choice):
    return [tuple(b for b, c in zip(bits, pick) if c) for pick in itertools.product(choice, repeat=len(bits))]


def prepare_kernel(
    n, owners, e_ref, first_ref, second_ref, scale_ref, inverse_ref, parts, counts, got, send_sems, recv_sems,
    send_counts, recv_counts
):
    me, home = lax.axis_index("code"), lax.axis_index("item")
    barrier = pltpu.get_barrier_semaphore()
    for step in range(1, n):
        pl.semaphore_signal(barrier, inc=1, device_id={"code": lax.rem(me + step, n)}, device_id_type=pl.DeviceIdType.MESH)
    for step in range(1, owners):
        pl.semaphore_signal(
            barrier, inc=1, device_id={"item": lax.rem(home + step, owners)}, device_id_type=pl.DeviceIdType.MESH
        )
    items = e_ref.shape[1]
    width = min(items, 8 * LANES)

    @pl.loop(0, items // width)
    def _(at):
        columns = pl.ds(pl.multiple_of(at * width, width), width)
        values = e_ref[:, columns].astype(jnp.float32)
        parts[0, :, columns] = jnp.sum(values * values, axis=0, keepdims=True)

    pl.semaphore_wait(barrier, n + owners - 2)
    copies = []
    for step in range(1, n):
        copy = pltpu.make_async_remote_copy(
            src_ref=parts.at[0],
            dst_ref=parts.at[step],
            send_sem=send_sems.at[step],
            recv_sem=recv_sems.at[step],
            device_id={"code": lax.rem(me + step, n)},
            device_id_type=pl.DeviceIdType.MESH,
        )
        copy.start()
        copies.append(copy)

    rows = counts.shape[2]
    high_of = lax.broadcasted_iota(jnp.int32, (owners * rows, width), 0)
    low_of = lax.broadcasted_iota(jnp.int32, (LANES, width), 0)
    for level, codes_ref in enumerate((first_ref, second_ref)):

        def add(at, total):
            codes = codes_ref[:, pl.ds(pl.multiple_of(at * width, width), width)]
            high = jnp.where(lax.shift_right_logical(codes, 7) == high_of, 1.0, 0.0).astype(jnp.bfloat16)
            low = jnp.where(lax.bitwise_and(codes, LANES - 1) == low_of, 1.0, 0.0).astype(jnp.bfloat16)
            return total + lax.dot_general(high, low, (((1,), (1,)), ((), ())), preferred_element_type=jnp.float32)

        total = lax.fori_loop(0, items // width, add, jnp.zeros((owners * rows, LANES), jnp.float32))
        for owner in range(owners):
            counts[owner, level] = total[owner * rows:(owner + 1) * rows]
    for step in range(1, owners):
        there = lax.rem(home + step, owners)
        copy = pltpu.make_async_remote_copy(
            src_ref=counts.at[there],
            dst_ref=got.at[step],
            send_sem=send_counts.at[step],
            recv_sem=recv_counts.at[step],
            device_id={"item": there},
            device_id_type=pl.DeviceIdType.MESH,
        )
        copy.start()
        copies.append(copy)
    for copy in copies[:n - 1]:
        copy.wait()
    squares = parts[0]
    for step in range(1, n):
        squares = squares + parts[step]
    scale_ref[...] = lax.rsqrt(squares / D + 1e-06)
    for copy in copies[n - 1:]:
        copy.wait()
    held = counts[home]
    for step in range(1, owners):
        held = held + got[step]
    inverse_ref[...] = 0.5 / (held + 1.0)


def prepare(embeddings, first_codes, second_codes, n, owners, total):
    items = embeddings.shape[1]
    rows = total // owners // LANES
    return pl.pallas_call(
        functools.partial(prepare_kernel, n, owners),
        out_shape=(
            jax.ShapeDtypeStruct((1, items), jnp.float32),
            jax.ShapeDtypeStruct((2, rows, LANES), jnp.float32),
        ),
        in_specs=[VMEM] * 3,
        out_specs=(VMEM, VMEM),
        scratch_shapes=[
            pltpu.VMEM((n, 1, items), jnp.float32),
            pltpu.VMEM((owners, 2, rows, LANES), jnp.float32),
            pltpu.VMEM((owners, 2, rows, LANES), jnp.float32),
            pltpu.SemaphoreType.DMA((n,)),
            pltpu.SemaphoreType.DMA((n,)),
            pltpu.SemaphoreType.DMA((owners,)),
            pltpu.SemaphoreType.DMA((owners,)),
        ],
        compiler_params=pltpu.CompilerParams(collective_id=0, has_side_effects=True, vmem_limit_bytes=16 * MIB),
        cost_estimate=pl.CostEstimate(flops=0, bytes_accessed=16 * MIB, transcendentals=0),
        name="prepare",
    )(embeddings, first_codes[None, :], second_codes[None, :])


def clear(piles):
    rows = piles[0].shape[0]
    step = min(rows, 64)

    @pl.loop(0, rows // step)
    def _(at):
        for pile in piles:
            pile[pl.ds(pl.multiple_of(at * step, step), step), :] = jnp.zeros((step, pile.shape[1]), pile.dtype)


def merge(piles):
    rows = piles[0].shape[0]
    step = min(rows, 64)

    @pl.loop(0, rows // step)
    def _(at):
        where = pl.ds(pl.multiple_of(at * step, step), step)
        parts = [pile[where, :] for pile in piles]
        while len(parts) > 1:
            parts = [a + b for a, b in zip(parts[::2], parts[1::2])]
        piles[0][where, :] = parts[0]


def add_rows(piles, codes, rows):
    held = [piles[at % PILES][pl.ds(code, 1), :] for at, code in enumerate(codes)]
    first = [held[at] + rows[at] for at in range(PILES)]
    second = [
        jnp.where(codes[at] == codes[at + PILES], first[at], held[at + PILES]) + rows[at + PILES] for at in range(PILES)
    ]
    for at in range(PILES):
        piles[at][pl.ds(codes[at], 1), :] = first[at]
    for at in range(PILES):
        piles[at][pl.ds(codes[at + PILES], 1), :] = second[at]


def first_kernel(codes_ref, e_ref, scale_ref, normed_ref, sums_ref, left, right, *more):
    piles = (sums_ref,) + more
    items = e_ref.shape[1]
    clear(piles)

    @pl.loop(0, items // (2 * LANES))
    def _(at):
        base = pl.multiple_of(at * 2 * LANES, 2 * LANES)
        for which, stage in enumerate((left, right)):
            span = pl.ds(pl.multiple_of(base + which * LANES, LANES), LANES)
            block = (e_ref[:, span].astype(jnp.float32) * scale_ref[:, span]).T
            stage[...] = block
            normed_ref[span, :] = block
        for which, stage in enumerate((left, right)):
            for start in range(0, LANES, GROUP):
                rows = [stage[start + j:start + j + 1, :] for j in range(GROUP)]
                add_rows(piles, [codes_ref[base + which * LANES + start + j] for j in range(GROUP)], rows)

    merge(piles)


def second_kernel(first_ref, second_ref, normed_ref, table_ref, middle_ref, sums_ref, *more):
    piles = (sums_ref,) + more
    items = normed_ref.shape[0]
    clear(piles)

    @pl.loop(0, items // SPAN)
    def _(at):
        for start in range(0, SPAN, GROUP):
            base = pl.multiple_of(at * SPAN + start, GROUP)
            rows = [
                normed_ref[pl.ds(base + j, 1), :] - table_ref[pl.ds(first_ref[base + j], 1), :] for j in range(GROUP)
            ]
            add_rows(piles, [second_ref[base + j] for j in range(GROUP)], rows)
            for j in range(GROUP):
                middle_ref[pl.ds(base + j, 1), :] = rows[j]

    merge(piles)


def last_kernel(block, codes_ref, middle_ref, table_ref, out_ref, left, right):
    start = pl.program_id(0) * block

    @pl.loop(0, block // (2 * LANES))
    def _(at):
        base = pl.multiple_of(at * 2 * LANES, 2 * LANES)
        for which, stage in enumerate((left, right)):
            for group in range(0, LANES, GROUP):
                rows = [
                    table_ref[pl.ds(codes_ref[start + base + which * LANES + group + j], 1), :] for j in range(GROUP)
                ]
                for j in range(GROUP):
                    stage[group + j:group + j + 1, :] = rows[j]
        for which, stage in enumerate((left, right)):
            span = pl.ds(pl.multiple_of(base + which * LANES, LANES), LANES)
            out_ref[:, span] = (middle_ref[span, :] - stage[...]).T


def exchange_kernel(n, sums_ref, old_ref, inverse_ref, whole_ref, own_ref, old, inverse, slots, send_in, recv_in, send_out, recv_out):
    levels = n.bit_length() - 1
    me = lax.axis_index("item")
    size = sums_ref.shape[0] // n
    half = size // 2
    rest = list(range(1, levels))
    orders = ([0] + rest, [0] + rest[::-1])

    def block(owner, path):
        return pl.ds(pl.multiple_of(owner * size + path * half, half), half)

    place_in, place_out = {}, {}
    for path, order in enumerate(orders):
        for step in range(levels):
            for far in subsets(order[step + 1:], (1, 0)):
                place_in[path, step, frozenset(far)] = len(place_in)
            for held in subsets(order[::-1][:step], (0, 1)):
                place_out[path, step, frozenset(held)] = len(place_out)

    sent = []

    def send_sum(path, step, far, source):
        slot = place_in[path, step, frozenset(far)]
        copy = pltpu.make_async_remote_copy(
            src_ref=source,
            dst_ref=slots.at[slot],
            send_sem=send_in.at[slot],
            recv_sem=recv_in.at[slot],
            device_id={"item": flip(me, [orders[path][step]])},
            device_id_type=pl.DeviceIdType.MESH,
        )
        copy.start()
        sent.append(copy)

    def new_copy(path, step, held, rows):
        slot = place_out[path, step, frozenset(held)]
        return pltpu.make_async_remote_copy(
            src_ref=whole_ref.at[rows],
            dst_ref=whole_ref.at[rows],
            send_sem=send_out.at[slot],
            recv_sem=recv_out.at[slot],
            device_id={"item": flip(me, [orders[path][::-1][step]])},
            device_id_type=pl.DeviceIdType.MESH,
        )

    def send_new(path, step, held):
        copy = new_copy(path, step, held, block(flip(me, held), path))
        copy.start()
        sent.append(copy)

    barrier = pltpu.get_barrier_semaphore()
    for bit in range(levels):
        pl.semaphore_signal(barrier, inc=1, device_id={"item": flip(me, [bit])}, device_id_type=pl.DeviceIdType.MESH)
    pl.semaphore_wait(barrier, levels)

    for fars in zip(*(subsets(order[1:], (1, 0)) for order in orders)):
        for path, far in enumerate(fars):
            send_sum(path, 0, far, sums_ref.at[block(flip(me, (0,) + far), path)])
    for at in range(size // LANES):
        span = slice(at * LANES, (at + 1) * LANES)
        old[span, :] = (0.5 * old_ref[:, span]).T
        inverse[span, :] = jnp.broadcast_to(inverse_ref[at:at + 1, :], (old.shape[1], LANES)).T
    for step in range(levels):
        for fars in zip(*(subsets(order[step + 1:], (1, 0)) for order in orders)):
            for path, far in enumerate(fars):
                slot = place_in[path, step, frozenset(far)]
                pltpu.make_async_remote_copy(
                    src_ref=slots.at[slot],
                    dst_ref=slots.at[slot],
                    send_sem=send_in.at[slot],
                    recv_sem=recv_in.at[slot],
                    device_id={"item": flip(me, [orders[path][step]])},
                    device_id_type=pl.DeviceIdType.MESH,
                ).wait_recv()
                if step == 0:
                    mine = sums_ref[block(flip(me, far), path), :]
                else:
                    mine = slots[place_in[path, step - 1, frozenset(far)]]
                total = slots[slot] + mine
                if step < levels - 1:
                    slots[slot] = total
                    ahead = orders[path][step + 1]
                    if ahead in far:
                        send_sum(path, step + 1, tuple(b for b in far if b != ahead), slots.at[slot])
                else:
                    rows = pl.ds(path * half, half)
                    new = old[rows, :] + total * inverse[rows, :]
                    whole_ref[block(me, path), :] = new
                    for later in range(levels):
                        send_new(path, later, ())
                    for at in range(half // LANES):
                        own_ref[:, path * half + at * LANES:path * half + (at + 1) * LANES] = new[
                            at * LANES:(at + 1) * LANES, :
                        ].T

    for step in range(levels):
        for helds in zip(*(subsets(order[::-1][:step], (0, 1)) for order in orders)):
            for path, held in enumerate(helds):
                got = held + (orders[path][::-1][step],)
                new_copy(path, step, held, block(flip(me, got), path)).wait_recv()
                for later in range(step + 1, levels):
                    send_new(path, later, got)
    for copy in sent:
        copy.wait_send()


def exchange(sums, old, inverse, n, collective_id):
    rows, width = sums.shape
    size = rows // n
    count = 2 * (n - 1)
    return pl.pallas_call(
        functools.partial(exchange_kernel, n),
        out_shape=(jax.ShapeDtypeStruct(sums.shape, jnp.float32), jax.ShapeDtypeStruct((width, size), jnp.float32)),
        in_specs=[VMEM] * 3,
        out_specs=(VMEM, VMEM),
        scratch_shapes=[
            pltpu.VMEM((size, width), jnp.float32),
            pltpu.VMEM((size, width), jnp.float32),
            pltpu.VMEM((count, size // 2, width), jnp.float32),
            pltpu.SemaphoreType.DMA((count,)),
            pltpu.SemaphoreType.DMA((count,)),
            pltpu.SemaphoreType.DMA((count,)),
            pltpu.SemaphoreType.DMA((count,)),
        ],
        compiler_params=pltpu.CompilerParams(
            collective_id=collective_id, has_side_effects=True, vmem_limit_bytes=18 * MIB
        ),
        cost_estimate=pl.CostEstimate(flops=0, bytes_accessed=128 * 2**20, transcendentals=0),
        name="exchange",
    )(sums, old, inverse)


def on_device(owners, feature_parts, embeddings, first_codes, second_codes, first_old, second_old):
    width, items = embeddings.shape
    total = first_old.shape[1] * owners
    f32 = jnp.float32
    cost = pl.CostEstimate(flops=0, bytes_accessed=64 * MIB, transcendentals=0)
    piles = [pltpu.VMEM((total, width), f32)] * (PILES - 1)
    row_sums = jax.ShapeDtypeStruct((total, width), f32)
    row_items = jax.ShapeDtypeStruct((items, width), f32)

    stage = pltpu.VMEM((LANES, width), f32)
    scales, inverse = prepare(embeddings, first_codes, second_codes, feature_parts, owners, total)
    normed, first_sums = pl.pallas_call(
        first_kernel,
        out_shape=(row_items, row_sums),
        in_specs=[SMEM, VMEM, VMEM],
        out_specs=(VMEM, VMEM),
        scratch_shapes=[stage, stage] + piles,
        compiler_params=pltpu.CompilerParams(vmem_limit_bytes=44 * MIB),
        cost_estimate=cost,
        name="first_sums",
    )(first_codes, embeddings, scales)
    first_whole, first_own = exchange(first_sums, first_old, inverse[0], owners, 1)
    middle, second_sums = pl.pallas_call(
        second_kernel,
        out_shape=(row_items, row_sums),
        in_specs=[SMEM, SMEM, VMEM, VMEM],
        out_specs=(VMEM, VMEM),
        scratch_shapes=piles,
        compiler_params=pltpu.CompilerParams(vmem_limit_bytes=48 * MIB),
        cost_estimate=cost,
        name="second_sums",
    )(first_codes, second_codes, normed, first_whole)
    second_whole, second_own = exchange(second_sums, second_old, inverse[1], owners, 2)
    block = min(items, 1024)
    leftover = pl.pallas_call(
        functools.partial(last_kernel, block),
        out_shape=jax.ShapeDtypeStruct((width, items), f32),
        grid=(items // block,),
        in_specs=[
            SMEM,
            pl.BlockSpec((block, width), lambda at: (at, 0)),
            pl.BlockSpec((total, width), lambda at: (0, 0)),
        ],
        out_specs=pl.BlockSpec((width, block), lambda at: (0, at)),
        scratch_shapes=[stage, stage],
        compiler_params=pltpu.CompilerParams(vmem_limit_bytes=20 * MIB),
        cost_estimate=cost,
        name="leftover",
    )(second_codes, middle, second_whole)
    return (first_own, second_own, leftover)


def solution(mesh):
    in_specs = (P("code", "item"), P("item"), P("item"), P("code", "item"), P("code", "item"))
    out_specs = (P("code", "item"), P("code", "item"), P("code", "item"))
    return jax.shard_map(
        functools.partial(on_device, mesh.shape["item"], mesh.shape["code"]),
        mesh=mesh,
        in_specs=in_specs,
        out_specs=out_specs,
        check_vma=False,
    )
```

```python
import functools
import itertools

import jax
import jax.numpy as jnp
from jax import lax
from jax.experimental import pallas as pl
from jax.experimental.pallas import tpu as pltpu
from jax.sharding import PartitionSpec as P

D = 512
LANES = 128
PILES = 8
GROUP = 2 * PILES
SPAN = 128
BLOCK = 1024
PATHS = 4
MIB = 2**20
VMEM_BYTES = 56 * MIB

VMEM = pl.BlockSpec(memory_space=pltpu.VMEM)
SMEM = pl.BlockSpec(memory_space=pltpu.SMEM)
ANY = pl.BlockSpec(memory_space=pl.ANY)


def flip(me, bits):
    other = me
    for bit in bits:
        weight = 2**bit
        other = other + weight - 2 * weight * lax.rem(lax.div(me, weight), 2)
    return other


def subsets(bits, choice):
    return [tuple(b for b, c in zip(bits, pick) if c) for pick in itertools.product(choice, repeat=len(bits))]


def prepare_kernel(
    n, owners, e_ref, first_ref, second_ref, scale_ref, inverse_ref, parts, counts, got, send_sems, recv_sems,
    send_counts, recv_counts
):
    me, home = lax.axis_index("code"), lax.axis_index("item")
    barrier = pltpu.get_barrier_semaphore()
    for step in range(1, n):
        pl.semaphore_signal(barrier, inc=1, device_id={"code": lax.rem(me + step, n)}, device_id_type=pl.DeviceIdType.MESH)
    for step in range(1, owners):
        pl.semaphore_signal(
            barrier, inc=1, device_id={"item": lax.rem(home + step, owners)}, device_id_type=pl.DeviceIdType.MESH
        )
    items = e_ref.shape[1]
    width = min(items, 8 * LANES)

    @pl.loop(0, items // width)
    def _(at):
        columns = pl.ds(pl.multiple_of(at * width, width), width)
        values = e_ref[:, columns].astype(jnp.float32)
        parts[0, :, columns] = jnp.sum(values * values, axis=0, keepdims=True)

    pl.semaphore_wait(barrier, n + owners - 2)
    copies = []
    for step in range(1, n):
        copy = pltpu.make_async_remote_copy(
            src_ref=parts.at[0],
            dst_ref=parts.at[step],
            send_sem=send_sems.at[step],
            recv_sem=recv_sems.at[step],
            device_id={"code": lax.rem(me + step, n)},
            device_id_type=pl.DeviceIdType.MESH,
        )
        copy.start()
        copies.append(copy)

    rows = counts.shape[2]
    high_of = lax.broadcasted_iota(jnp.int32, (owners * rows, width), 0)
    low_of = lax.broadcasted_iota(jnp.int32, (LANES, width), 0)
    for level, codes_ref in enumerate((first_ref, second_ref)):

        def add(at, total):
            codes = codes_ref[:, pl.ds(pl.multiple_of(at * width, width), width)]
            high = jnp.where(lax.shift_right_logical(codes, 7) == high_of, 1.0, 0.0).astype(jnp.bfloat16)
            low = jnp.where(lax.bitwise_and(codes, LANES - 1) == low_of, 1.0, 0.0).astype(jnp.bfloat16)
            return total + lax.dot_general(high, low, (((1,), (1,)), ((), ())), preferred_element_type=jnp.float32)

        total = lax.fori_loop(0, items // width, add, jnp.zeros((owners * rows, LANES), jnp.float32))
        for owner in range(owners):
            counts[owner, level] = total[owner * rows:(owner + 1) * rows]
    for step in range(1, owners):
        there = lax.rem(home + step, owners)
        copy = pltpu.make_async_remote_copy(
            src_ref=counts.at[there],
            dst_ref=got.at[step],
            send_sem=send_counts.at[step],
            recv_sem=recv_counts.at[step],
            device_id={"item": there},
            device_id_type=pl.DeviceIdType.MESH,
        )
        copy.start()
        copies.append(copy)
    for copy in copies[:n - 1]:
        copy.wait()
    squares = parts[0]
    for step in range(1, n):
        squares = squares + parts[step]
    scale_ref[...] = lax.rsqrt(squares / D + 1e-06)
    for copy in copies[n - 1:]:
        copy.wait()
    held = counts[home]
    for step in range(1, owners):
        held = held + got[step]
    inverse_ref[...] = 0.5 / (held + 1.0)


def prepare(embeddings, first_codes, second_codes, n, owners, total):
    items = embeddings.shape[1]
    rows = total // owners // LANES
    return pl.pallas_call(
        functools.partial(prepare_kernel, n, owners),
        out_shape=(
            jax.ShapeDtypeStruct((1, items), jnp.float32),
            jax.ShapeDtypeStruct((2, rows, LANES), jnp.float32),
        ),
        in_specs=[VMEM] * 3,
        out_specs=(VMEM, VMEM),
        scratch_shapes=[
            pltpu.VMEM((n, 1, items), jnp.float32),
            pltpu.VMEM((owners, 2, rows, LANES), jnp.float32),
            pltpu.VMEM((owners, 2, rows, LANES), jnp.float32),
            pltpu.SemaphoreType.DMA((n,)),
            pltpu.SemaphoreType.DMA((n,)),
            pltpu.SemaphoreType.DMA((owners,)),
            pltpu.SemaphoreType.DMA((owners,)),
        ],
        compiler_params=pltpu.CompilerParams(collective_id=0, has_side_effects=True, vmem_limit_bytes=VMEM_BYTES),
        cost_estimate=pl.CostEstimate(flops=0, bytes_accessed=16 * MIB, transcendentals=0),
        name="prepare",
    )(embeddings, first_codes[None, :], second_codes[None, :])


def clear(piles):
    rows = piles[0].shape[0]
    step = min(rows, 64)

    @pl.loop(0, rows // step)
    def _(at):
        for pile in piles:
            pile[pl.ds(pl.multiple_of(at * step, step), step), :] = jnp.zeros((step, pile.shape[1]), pile.dtype)


def merge(piles):
    rows = piles[0].shape[0]
    step = min(rows, 64)

    @pl.loop(0, rows // step)
    def _(at):
        where = pl.ds(pl.multiple_of(at * step, step), step)
        parts = [pile[where, :] for pile in piles]
        while len(parts) > 1:
            parts = [a + b for a, b in zip(parts[::2], parts[1::2])]
        piles[0][where, :] = parts[0]


def add_rows(piles, codes, rows):
    held = [piles[at % PILES][pl.ds(code, 1), :] for at, code in enumerate(codes)]
    first = [held[at] + rows[at] for at in range(PILES)]
    second = [
        jnp.where(codes[at] == codes[at + PILES], first[at], held[at + PILES]) + rows[at + PILES] for at in range(PILES)
    ]
    for at in range(PILES):
        piles[at][pl.ds(codes[at], 1), :] = first[at]
    for at in range(PILES):
        piles[at][pl.ds(codes[at + PILES], 1), :] = second[at]


def first_kernel(codes_ref, e_ref, scale_ref, normed_ref, sums_ref, left, right, *more):
    piles = (sums_ref,) + more
    items = e_ref.shape[1]
    offset = pl.program_id(0) * items

    @pl.when(pl.program_id(0) == 0)
    def _():
        clear(piles)

    @pl.loop(0, items // (2 * LANES))
    def _(at):
        base = pl.multiple_of(at * 2 * LANES, 2 * LANES)
        for which, stage in enumerate((left, right)):
            span = pl.ds(pl.multiple_of(base + which * LANES, LANES), LANES)
            block = (e_ref[:, span].astype(jnp.float32) * scale_ref[:, span]).T
            stage[...] = block
            normed_ref[span, :] = block
        for which, stage in enumerate((left, right)):
            for start in range(0, LANES, GROUP):
                rows = [stage[start + j:start + j + 1, :] for j in range(GROUP)]
                add_rows(piles, [codes_ref[offset + base + which * LANES + start + j] for j in range(GROUP)], rows)

    @pl.when(pl.program_id(0) == pl.num_programs(0) - 1)
    def _():
        merge(piles)


def second_kernel(first_ref, second_ref, normed_ref, table_ref, own_ref, middle_ref, sums_ref, new_ref, *more):
    piles = (sums_ref,) + more
    items = normed_ref.shape[0]
    offset = pl.program_id(0) * items

    @pl.when(pl.program_id(0) == 0)
    def _():
        new_ref[...] = own_ref[...]
        clear(piles)

    @pl.loop(0, items // SPAN)
    def _(at):
        for start in range(0, SPAN, GROUP):
            base = pl.multiple_of(at * SPAN + start, GROUP)
            rows = [
                normed_ref[pl.ds(base + j, 1), :] - table_ref[pl.ds(first_ref[offset + base + j], 1), :]
                for j in range(GROUP)
            ]
            add_rows(piles, [second_ref[offset + base + j] for j in range(GROUP)], rows)
            for j in range(GROUP):
                middle_ref[pl.ds(base + j, 1), :] = rows[j]

    @pl.when(pl.program_id(0) == pl.num_programs(0) - 1)
    def _():
        merge(piles)


def last_kernel(codes_ref, middle_ref, table_ref, own_ref, out_ref, new_ref, left, right):
    block = middle_ref.shape[0]
    start = pl.program_id(0) * block

    @pl.when(pl.program_id(0) == 0)
    def _():
        new_ref[...] = own_ref[...]

    @pl.loop(0, block // (2 * LANES))
    def _(at):
        base = pl.multiple_of(at * 2 * LANES, 2 * LANES)
        for which, stage in enumerate((left, right)):
            for group in range(0, LANES, GROUP):
                rows = [
                    table_ref[pl.ds(codes_ref[start + base + which * LANES + group + j], 1), :] for j in range(GROUP)
                ]
                for j in range(GROUP):
                    stage[group + j:group + j + 1, :] = rows[j]
        for which, stage in enumerate((left, right)):
            span = pl.ds(pl.multiple_of(base + which * LANES, LANES), LANES)
            out_ref[:, span] = (middle_ref[span, :] - stage[...]).T


def exchange_kernel(
    n, sums_ref, old_ref, inverse_ref, whole_ref, own_ref, old, inverse, fresh, kept, slots,
    keep_sems, own_sems, send_in, recv_in, send_out, recv_out
):
    levels = n.bit_length() - 1
    me = lax.axis_index("item")
    size = sums_ref.shape[0] // n
    part = size // PATHS
    rest = list(range(1, levels))
    orders = [[0] + (rest if path % 2 == 0 else rest[::-1]) for path in range(PATHS)]

    def block(owner, path):
        return pl.ds(pl.multiple_of(owner * size + path * part, part), part)

    place_in, place_out = {}, {}
    for path, order in enumerate(orders):
        for step in range(levels):
            for far in subsets(order[step + 1:], (1, 0)):
                place_in[path, step, frozenset(far)] = len(place_in)
            for held in subsets(order[::-1][:step], (0, 1)):
                place_out[path, step, frozenset(held)] = len(place_out)
    place_kept = {
        (path, frozenset(far)): at
        for at, (path, far) in enumerate(
            (path, far) for path in range(PATHS) for far in subsets(orders[path][1:], (1, 0))
        )
    }
    sent = []

    def sum_copy(path, step, far, source):
        slot = place_in[path, step, frozenset(far)]
        return pltpu.make_async_remote_copy(
            src_ref=source,
            dst_ref=slots.at[slot],
            send_sem=send_in.at[slot],
            recv_sem=recv_in.at[slot],
            device_id={"item": flip(me, [orders[path][step]])},
            device_id_type=pl.DeviceIdType.MESH,
        )

    def new_copy(path, step, held, source, rows):
        slot = place_out[path, step, frozenset(held)]
        return pltpu.make_async_remote_copy(
            src_ref=source,
            dst_ref=whole_ref.at[rows],
            send_sem=send_out.at[slot],
            recv_sem=recv_out.at[slot],
            device_id={"item": flip(me, [orders[path][::-1][step]])},
            device_id_type=pl.DeviceIdType.MESH,
        )

    def send(copy):
        copy.start()
        sent.append(copy)

    def keep_copy(path, far):
        slot = place_kept[path, frozenset(far)]
        return pltpu.make_async_copy(sums_ref.at[block(flip(me, far), path)], kept.at[slot], keep_sems.at[slot])

    def fars_of(step):
        return list(zip(*(subsets(order[step + 1:], (1, 0)) for order in orders)))

    def open_with(fars):
        for path, far in enumerate(fars):
            send(sum_copy(path, 0, far, sums_ref.at[block(flip(me, (0,) + far), path)]))

    barrier = pltpu.get_barrier_semaphore()
    for bit in range(levels):
        pl.semaphore_signal(barrier, inc=1, device_id={"item": flip(me, [bit])}, device_id_type=pl.DeviceIdType.MESH)
    for fars in fars_of(0):
        for path, far in enumerate(fars):
            keep_copy(path, far).start()
    pl.semaphore_wait(barrier, levels)

    opening = fars_of(0)
    middle = len(opening) // 2
    for fars in opening[:middle]:
        open_with(fars)
    for step in range(levels):
        for at, fars in enumerate(fars_of(step)):
            if step == 0 and at == middle:
                for later in opening[middle:]:
                    open_with(later)
            for path, far in enumerate(fars):
                slot = place_in[path, step, frozenset(far)]
                sum_copy(path, step, far, slots.at[slot]).wait_recv()
                if step == 0:
                    keep_copy(path, far).wait()
                    mine = kept[place_kept[path, frozenset(far)]]
                else:
                    mine = slots[place_in[path, step - 1, frozenset(far)]]
                total = slots[slot] + mine
                if step < levels - 1:
                    slots[slot] = total
                    ahead = orders[path][step + 1]
                    if ahead in far:
                        send(sum_copy(path, step + 1, tuple(b for b in far if b != ahead), slots.at[slot]))
                else:
                    rows = pl.ds(path * part, part)
                    fresh[rows, :] = old[rows, :] + total * inverse[rows, :]
                    for later in range(levels):
                        send(new_copy(path, later, (), fresh.at[rows], block(me, path)))
                    pltpu.make_async_copy(fresh.at[rows], whole_ref.at[block(me, path)], own_sems.at[path]).start()
        if step == 0:
            for at in range(size // LANES):
                span = slice(at * LANES, (at + 1) * LANES)
                old[span, :] = (0.5 * old_ref[:, span]).T
                inverse[span, :] = jnp.broadcast_to(inverse_ref[at:at + 1, :], (old.shape[1], LANES)).T

    for step in range(levels):
        for helds in zip(*(subsets(order[::-1][:step], (0, 1)) for order in orders)):
            for path, held in enumerate(helds):
                got = held + (orders[path][::-1][step],)
                rows = block(flip(me, got), path)
                new_copy(path, step, held, whole_ref.at[rows], rows).wait_recv()
                for later in range(step + 1, levels):
                    send(new_copy(path, later, got, whole_ref.at[rows], rows))
        if step == 0:
            for at in range(size // LANES):
                span = slice(at * LANES, (at + 1) * LANES)
                own_ref[:, span] = fresh[span, :].T
    for path in range(PATHS):
        pltpu.make_async_copy(
            fresh.at[pl.ds(path * part, part)], whole_ref.at[block(me, path)], own_sems.at[path]
        ).wait()
    for copy in sent:
        copy.wait_send()


def exchange(sums, old, inverse, n, collective_id):
    rows, width = sums.shape
    size = rows // n
    part = size // PATHS
    count = PATHS * (n - 1)
    return pl.pallas_call(
        functools.partial(exchange_kernel, n),
        out_shape=(jax.ShapeDtypeStruct(sums.shape, jnp.float32), jax.ShapeDtypeStruct((width, size), jnp.float32)),
        in_specs=[ANY, VMEM, VMEM],
        out_specs=(ANY, VMEM),
        scratch_shapes=[
            pltpu.VMEM((size, width), jnp.float32),
            pltpu.VMEM((size, width), jnp.float32),
            pltpu.VMEM((size, width), jnp.float32),
            pltpu.VMEM((PATHS * n // 2, part, width), jnp.float32),
            pltpu.VMEM((count, part, width), jnp.float32),
            pltpu.SemaphoreType.DMA((PATHS * n // 2,)),
            pltpu.SemaphoreType.DMA((PATHS,)),
            pltpu.SemaphoreType.DMA((count,)),
            pltpu.SemaphoreType.DMA((count,)),
            pltpu.SemaphoreType.DMA((count,)),
            pltpu.SemaphoreType.DMA((count,)),
        ],
        compiler_params=pltpu.CompilerParams(
            collective_id=collective_id, has_side_effects=True, vmem_limit_bytes=VMEM_BYTES
        ),
        cost_estimate=pl.CostEstimate(flops=0, bytes_accessed=128 * MIB, transcendentals=0),
        name="exchange",
    )(sums, old, inverse)


def on_device(owners, feature_parts, embeddings, first_codes, second_codes, first_old, second_old):
    width, items = embeddings.shape
    total = first_old.shape[1] * owners
    f32 = jnp.float32
    cost = pl.CostEstimate(flops=0, bytes_accessed=64 * MIB, transcendentals=0)
    piles = [pltpu.VMEM((total, width), f32)] * (PILES - 1)
    row_sums = jax.ShapeDtypeStruct((total, width), f32)
    row_items = jax.ShapeDtypeStruct((items, width), f32)

    stage = pltpu.VMEM((LANES, width), f32)
    scales, inverse = prepare(embeddings, first_codes, second_codes, feature_parts, owners, total)
    block = min(items, BLOCK)
    steps = (items // block,)
    local = pltpu.CompilerParams(vmem_limit_bytes=VMEM_BYTES)
    by_rows = pl.BlockSpec((block, width), lambda at: (at, 0))
    by_columns = pl.BlockSpec((width, block), lambda at: (0, at))
    table = pl.BlockSpec((total, width), lambda at: (0, 0))
    own = pl.BlockSpec(first_old.shape, lambda at: (0, 0))
    own_shape = jax.ShapeDtypeStruct(first_old.shape, f32)
    normed, first_sums = pl.pallas_call(
        first_kernel,
        out_shape=(row_items, row_sums),
        grid=steps,
        in_specs=[SMEM, by_columns, pl.BlockSpec((1, block), lambda at: (0, at))],
        out_specs=(by_rows, table),
        scratch_shapes=[stage, stage] + piles,
        compiler_params=local,
        cost_estimate=cost,
        name="first_sums",
    )(first_codes, embeddings, scales)
    first_whole, first_own = exchange(first_sums, first_old, inverse[0], owners, 1)
    middle, second_sums, first_new = pl.pallas_call(
        second_kernel,
        out_shape=(row_items, row_sums, own_shape),
        grid=steps,
        in_specs=[SMEM, SMEM, by_rows, table, own],
        out_specs=(by_rows, table, own),
        scratch_shapes=piles,
        compiler_params=local,
        cost_estimate=cost,
        name="second_sums",
    )(first_codes, second_codes, normed, first_whole, first_own)
    second_whole, second_own = exchange(second_sums, second_old, inverse[1], owners, 2)
    leftover, second_new = pl.pallas_call(
        last_kernel,
        out_shape=(jax.ShapeDtypeStruct((width, items), f32), own_shape),
        grid=steps,
        in_specs=[SMEM, by_rows, table, own],
        out_specs=(by_columns, own),
        scratch_shapes=[stage, stage],
        compiler_params=local,
        cost_estimate=cost,
        name="leftover",
    )(second_codes, middle, second_whole, second_own)
    return (first_new, second_new, leftover)


def solution(mesh):
    in_specs = (P("code", "item"), P("item"), P("item"), P("code", "item"), P("code", "item"))
    out_specs = (P("code", "item"), P("code", "item"), P("code", "item"))
    return jax.shard_map(
        functools.partial(on_device, mesh.shape["item"], mesh.shape["code"]),
        mesh=mesh,
        in_specs=in_specs,
        out_specs=out_specs,
        check_vma=False,
    )
```

```python
import functools
import itertools

import jax
import jax.numpy as jnp
from jax import lax
from jax.experimental import pallas as pl
from jax.experimental.pallas import tpu as pltpu
from jax.sharding import PartitionSpec as P

D = 512
LANES = 128
PILES = 8
GROUP = 2 * PILES
SPAN = 128
BLOCK = 1024
PATHS = 4
MIB = 2**20
VMEM_BYTES = 56 * MIB

VMEM = pl.BlockSpec(memory_space=pltpu.VMEM)
SMEM = pl.BlockSpec(memory_space=pltpu.SMEM)
ANY = pl.BlockSpec(memory_space=pl.ANY)


def flip(me, bits):
    other = me
    for bit in bits:
        weight = 2**bit
        other = other + weight - 2 * weight * lax.rem(lax.div(me, weight), 2)
    return other


def subsets(bits, choice):
    return [tuple(b for b, c in zip(bits, pick) if c) for pick in itertools.product(choice, repeat=len(bits))]


def scales_kernel(n, e_ref, scale_ref, parts, send_sems, recv_sems):
    me = lax.axis_index("code")
    barrier = pltpu.get_barrier_semaphore()
    for step in range(1, n):
        pl.semaphore_signal(barrier, inc=1, device_id={"code": lax.rem(me + step, n)}, device_id_type=pl.DeviceIdType.MESH)
    items = e_ref.shape[1]
    width = min(items, 8 * LANES)

    @pl.loop(0, items // width)
    def _(at):
        columns = pl.ds(pl.multiple_of(at * width, width), width)
        values = e_ref[:, columns].astype(jnp.float32)
        parts[0, :, columns] = jnp.sum(values * values, axis=0, keepdims=True)

    pl.semaphore_wait(barrier, n - 1)
    copies = []
    for step in range(1, n):
        copy = pltpu.make_async_remote_copy(
            src_ref=parts.at[0],
            dst_ref=parts.at[step],
            send_sem=send_sems.at[step],
            recv_sem=recv_sems.at[step],
            device_id={"code": lax.rem(me + step, n)},
            device_id_type=pl.DeviceIdType.MESH,
        )
        copy.start()
        copies.append(copy)
    for copy in copies:
        copy.wait()
    squares = parts[0]
    for step in range(1, n):
        squares = squares + parts[step]
    scale_ref[...] = lax.rsqrt(squares / D + 1e-06)


def scales_of(embeddings, n):
    items = embeddings.shape[1]
    return pl.pallas_call(
        functools.partial(scales_kernel, n),
        out_shape=jax.ShapeDtypeStruct((1, items), jnp.float32),
        in_specs=[VMEM],
        out_specs=VMEM,
        scratch_shapes=[
            pltpu.VMEM((n, 1, items), jnp.float32),
            pltpu.SemaphoreType.DMA((n,)),
            pltpu.SemaphoreType.DMA((n,)),
        ],
        compiler_params=pltpu.CompilerParams(collective_id=0, has_side_effects=True, vmem_limit_bytes=VMEM_BYTES),
        cost_estimate=pl.CostEstimate(flops=0, bytes_accessed=16 * MIB, transcendentals=0),
        name="scales",
    )(embeddings)


def count_codes(codes_ref, total):
    items = codes_ref.shape[1]
    width = min(items, 8 * LANES)
    high_of = lax.broadcasted_iota(jnp.int32, (total // LANES, width), 0)
    low_of = lax.broadcasted_iota(jnp.int32, (LANES, width), 0)

    def add(at, held):
        codes = codes_ref[:, pl.ds(pl.multiple_of(at * width, width), width)]
        high = jnp.where(lax.shift_right_logical(codes, 7) == high_of, 1.0, 0.0).astype(jnp.bfloat16)
        low = jnp.where(lax.bitwise_and(codes, LANES - 1) == low_of, 1.0, 0.0).astype(jnp.bfloat16)
        return held + lax.dot_general(high, low, (((1,), (1,)), ((), ())), preferred_element_type=jnp.float32)

    return lax.fori_loop(0, items // width, add, jnp.zeros((total // LANES, LANES), jnp.float32))


def clear(piles):
    rows = piles[0].shape[0]
    step = min(rows, 128)

    @pl.loop(0, rows // step)
    def _(at):
        for pile in piles:
            pile[pl.ds(pl.multiple_of(at * step, step), step), :] = jnp.zeros((step, pile.shape[1]), pile.dtype)


def merge(piles):
    rows = piles[0].shape[0]
    step = min(rows, 128)

    @pl.loop(0, rows // step)
    def _(at):
        where = pl.ds(pl.multiple_of(at * step, step), step)
        parts = [pile[where, :] for pile in piles]
        while len(parts) > 1:
            parts = [a + b for a, b in zip(parts[::2], parts[1::2])]
        piles[0][where, :] = parts[0]


def add_rows(piles, codes, rows):
    held = [piles[at % PILES][pl.ds(code, 1), :] for at, code in enumerate(codes)]
    first = [held[at] + rows[at] for at in range(PILES)]
    second = [
        jnp.where(codes[at] == codes[at + PILES], first[at], held[at + PILES]) + rows[at + PILES] for at in range(PILES)
    ]
    for at in range(PILES):
        piles[at][pl.ds(codes[at], 1), :] = first[at]
        piles[at][pl.ds(codes[at + PILES], 1), :] = second[at]


def first_kernel(codes_ref, e_ref, scale_ref, normed_ref, sums_ref, left, right, *more):
    piles = (sums_ref,) + more
    items = e_ref.shape[1]
    offset = pl.program_id(0) * items

    @pl.when(pl.program_id(0) == 0)
    def _():
        clear(piles)

    @pl.loop(0, items // (2 * LANES))
    def _(at):
        base = pl.multiple_of(at * 2 * LANES, 2 * LANES)
        for which, stage in enumerate((left, right)):
            span = pl.ds(pl.multiple_of(base + which * LANES, LANES), LANES)
            block = (e_ref[:, span].astype(jnp.float32) * scale_ref[:, span]).T
            stage[...] = block
            normed_ref[span, :] = block
        for which, stage in enumerate((left, right)):
            for start in range(0, LANES, GROUP):
                rows = [stage[start + j:start + j + 1, :] for j in range(GROUP)]
                add_rows(piles, [codes_ref[offset + base + which * LANES + start + j] for j in range(GROUP)], rows)

    @pl.when(pl.program_id(0) == pl.num_programs(0) - 1)
    def _():
        merge(piles)


def second_kernel(first_ref, second_ref, normed_ref, table_ref, own_ref, middle_ref, sums_ref, new_ref, *more):
    piles = (sums_ref,) + more
    items = normed_ref.shape[0]
    offset = pl.program_id(0) * items

    @pl.when(pl.program_id(0) == 0)
    def _():
        new_ref[...] = own_ref[...]
        clear(piles)

    @pl.loop(0, items // SPAN)
    def _(at):
        for start in range(0, SPAN, GROUP):
            base = pl.multiple_of(at * SPAN + start, GROUP)
            rows = [
                normed_ref[pl.ds(base + j, 1), :] - table_ref[pl.ds(first_ref[offset + base + j], 1), :]
                for j in range(GROUP)
            ]
            add_rows(piles, [second_ref[offset + base + j] for j in range(GROUP)], rows)
            for j in range(GROUP):
                middle_ref[pl.ds(base + j, 1), :] = rows[j]

    @pl.when(pl.program_id(0) == pl.num_programs(0) - 1)
    def _():
        merge(piles)


def last_kernel(codes_ref, middle_ref, table_ref, own_ref, out_ref, new_ref, left, right):
    block = middle_ref.shape[0]
    start = pl.program_id(0) * block

    @pl.when(pl.program_id(0) == 0)
    def _():
        new_ref[...] = own_ref[...]

    @pl.loop(0, block // (2 * LANES))
    def _(at):
        base = pl.multiple_of(at * 2 * LANES, 2 * LANES)
        for which, stage in enumerate((left, right)):
            for group in range(0, LANES, GROUP):
                rows = [
                    table_ref[pl.ds(codes_ref[start + base + which * LANES + group + j], 1), :] for j in range(GROUP)
                ]
                for j in range(GROUP):
                    stage[group + j:group + j + 1, :] = rows[j]
        for which, stage in enumerate((left, right)):
            span = pl.ds(pl.multiple_of(base + which * LANES, LANES), LANES)
            out_ref[:, span] = (middle_ref[span, :] - stage[...]).T


def exchange_kernel(n, counting, sums_ref, old_ref, *refs):
    if counting:
        *codes_refs, whole_ref, own_ref, inverse_ref = refs[:5]
        counts, got, send_counts, recv_counts = refs[-4:]
        refs = refs[5:-4]
    else:
        inverse_ref, whole_ref, own_ref = refs[:3]
        refs = refs[3:]
    old, inverse, fresh, kept, slots, keep_sems, own_sems, send_in, recv_in, send_out, recv_out = refs
    levels = n.bit_length() - 1
    me = lax.axis_index("item")
    size = sums_ref.shape[0] // n
    part = size // PATHS
    rest = list(range(1, levels))
    orders = [[0] + (rest if path % 2 == 0 else rest[::-1]) for path in range(PATHS)]

    def block(owner, path):
        return pl.ds(pl.multiple_of(owner * size + path * part, part), part)

    place_in, place_out = {}, {}
    for path, order in enumerate(orders):
        for step in range(levels):
            for far in subsets(order[step + 1:], (1, 0)):
                place_in[path, step, frozenset(far)] = len(place_in)
            for held in subsets(order[::-1][:step], (0, 1)):
                place_out[path, step, frozenset(held)] = len(place_out)
    place_kept = {
        (path, frozenset(far)): at
        for at, (path, far) in enumerate(
            (path, far) for path in range(PATHS) for far in subsets(orders[path][1:], (1, 0))
        )
    }
    sent = []

    def sum_copy(path, step, far, source):
        slot = place_in[path, step, frozenset(far)]
        return pltpu.make_async_remote_copy(
            src_ref=source,
            dst_ref=slots.at[slot],
            send_sem=send_in.at[slot],
            recv_sem=recv_in.at[slot],
            device_id={"item": flip(me, [orders[path][step]])},
            device_id_type=pl.DeviceIdType.MESH,
        )

    def new_copy(path, step, held, source, rows):
        slot = place_out[path, step, frozenset(held)]
        return pltpu.make_async_remote_copy(
            src_ref=source,
            dst_ref=whole_ref.at[rows],
            send_sem=send_out.at[slot],
            recv_sem=recv_out.at[slot],
            device_id={"item": flip(me, [orders[path][::-1][step]])},
            device_id_type=pl.DeviceIdType.MESH,
        )

    def send(copy):
        copy.start()
        sent.append(copy)

    def keep_copy(path, far):
        slot = place_kept[path, frozenset(far)]
        return pltpu.make_async_copy(sums_ref.at[block(flip(me, far), path)], kept.at[slot], keep_sems.at[slot])

    def fars_of(step):
        return list(zip(*(subsets(order[step + 1:], (1, 0)) for order in orders)))

    def open_with(fars):
        for path, far in enumerate(fars):
            send(sum_copy(path, 0, far, sums_ref.at[block(flip(me, (0,) + far), path)]))

    def count_copy(step):
        there = lax.rem(me + step, n)
        return pltpu.make_async_remote_copy(
            src_ref=counts.at[there],
            dst_ref=got.at[step],
            send_sem=send_counts.at[step],
            recv_sem=recv_counts.at[step],
            device_id={"item": there},
            device_id_type=pl.DeviceIdType.MESH,
        )

    def spread(level_inverse):
        for at in range(size // LANES):
            span = slice(at * LANES, (at + 1) * LANES)
            inverse[span, :] = jnp.broadcast_to(level_inverse[at:at + 1, :], (old.shape[1], LANES)).T

    barrier = pltpu.get_barrier_semaphore()
    if counting:
        peers = [lax.rem(me + step, n) for step in range(1, n)]
    else:
        peers = [flip(me, [bit]) for bit in range(levels)]
    for peer in peers:
        pl.semaphore_signal(barrier, inc=1, device_id={"item": peer}, device_id_type=pl.DeviceIdType.MESH)
    for fars in fars_of(0):
        for path, far in enumerate(fars):
            keep_copy(path, far).start()
    pl.semaphore_wait(barrier, len(peers))

    opening = fars_of(0)
    middle = len(opening) // 2
    for fars in opening[:middle]:
        open_with(fars)
    for step in range(levels):
        for at, fars in enumerate(fars_of(step)):
            if step == 0 and at == middle:
                for later in opening[middle:]:
                    open_with(later)
            for path, far in enumerate(fars):
                slot = place_in[path, step, frozenset(far)]
                sum_copy(path, step, far, slots.at[slot]).wait_recv()
                if step == 0:
                    keep_copy(path, far).wait()
                    mine = kept[place_kept[path, frozenset(far)]]
                else:
                    mine = slots[place_in[path, step - 1, frozenset(far)]]
                total = slots[slot] + mine
                if step < levels - 1:
                    slots[slot] = total
                    ahead = orders[path][step + 1]
                    if ahead in far:
                        send(sum_copy(path, step + 1, tuple(b for b in far if b != ahead), slots.at[slot]))
                else:
                    rows = pl.ds(path * part, part)
                    fresh[rows, :] = old[rows, :] + total * inverse[rows, :]
                    send(new_copy(path, 0, (), fresh.at[rows], block(me, path)))
                    pltpu.make_async_copy(fresh.at[rows], whole_ref.at[block(me, path)], own_sems.at[path]).start()
        if step == 0:
            for at in range(size // LANES):
                span = slice(at * LANES, (at + 1) * LANES)
                old[span, :] = (0.5 * old_ref[:, span]).T
            if counting:
                rows = counts.shape[2]
                for level, codes_ref in enumerate(codes_refs):
                    held = count_codes(codes_ref, n * size)
                    for owner in range(n):
                        counts[owner, level] = held[owner * rows:(owner + 1) * rows]
                for away in range(1, n):
                    send(count_copy(away))
            else:
                spread(inverse_ref[...])
        if step == levels - 2 and counting:
            held = counts[me]
            for away in range(1, n):
                count_copy(away).wait_recv()
                held = held + got[away]
            both = 0.5 / (held + 1.0)
            spread(both[0])
            inverse_ref[...] = both[1]
    for later in range(1, levels):
        for path in range(PATHS):
            send(new_copy(path, later, (), fresh.at[pl.ds(path * part, part)], block(me, path)))

    for step in range(levels):
        for helds in zip(*(subsets(order[::-1][:step], (0, 1)) for order in orders)):
            for path, held in enumerate(helds):
                got = held + (orders[path][::-1][step],)
                rows = block(flip(me, got), path)
                new_copy(path, step, held, whole_ref.at[rows], rows).wait_recv()
                for later in range(step + 1, levels):
                    send(new_copy(path, later, got, whole_ref.at[rows], rows))
        if step == 0:
            for at in range(size // LANES):
                span = slice(at * LANES, (at + 1) * LANES)
                own_ref[:, span] = fresh[span, :].T
    for path in range(PATHS):
        pltpu.make_async_copy(
            fresh.at[pl.ds(path * part, part)], whole_ref.at[block(me, path)], own_sems.at[path]
        ).wait()
    for copy in sent:
        copy.wait_send()


def exchange(sums, old, n, collective_id, inverse=None, codes=()):
    rows, width = sums.shape
    size = rows // n
    part = size // PATHS
    count = PATHS * (n - 1)
    out_shape = [jax.ShapeDtypeStruct(sums.shape, jnp.float32), jax.ShapeDtypeStruct((width, size), jnp.float32)]
    scratch = [
        pltpu.VMEM((size, width), jnp.float32),
        pltpu.VMEM((size, width), jnp.float32),
        pltpu.VMEM((size, width), jnp.float32),
        pltpu.VMEM((PATHS * n // 2, part, width), jnp.float32),
        pltpu.VMEM((count, part, width), jnp.float32),
        pltpu.SemaphoreType.DMA((PATHS * n // 2,)),
        pltpu.SemaphoreType.DMA((PATHS,)),
        pltpu.SemaphoreType.DMA((count,)),
        pltpu.SemaphoreType.DMA((count,)),
        pltpu.SemaphoreType.DMA((count,)),
        pltpu.SemaphoreType.DMA((count,)),
    ]
    if codes:
        inputs = (sums, old) + tuple(level[None, :] for level in codes)
        out_shape.append(jax.ShapeDtypeStruct((size // LANES, LANES), jnp.float32))
        scratch += [pltpu.VMEM((n, len(codes), size // LANES, LANES), jnp.float32)] * 2
        scratch += [pltpu.SemaphoreType.DMA((n,))] * 2
    else:
        inputs = (sums, old, inverse)
    return pl.pallas_call(
        functools.partial(exchange_kernel, n, bool(codes)),
        out_shape=out_shape,
        in_specs=[ANY] + [VMEM] * (len(inputs) - 1),
        out_specs=[ANY] + [VMEM] * (len(out_shape) - 1),
        scratch_shapes=scratch,
        compiler_params=pltpu.CompilerParams(
            collective_id=collective_id, has_side_effects=True, vmem_limit_bytes=VMEM_BYTES
        ),
        cost_estimate=pl.CostEstimate(flops=0, bytes_accessed=128 * MIB, transcendentals=0),
        name="exchange",
    )(*inputs)


def on_device(owners, feature_parts, embeddings, first_codes, second_codes, first_old, second_old):
    width, items = embeddings.shape
    total = first_old.shape[1] * owners
    f32 = jnp.float32
    cost = pl.CostEstimate(flops=0, bytes_accessed=64 * MIB, transcendentals=0)
    piles = [pltpu.VMEM((total, width), f32)] * (PILES - 1)
    row_sums = jax.ShapeDtypeStruct((total, width), f32)
    row_items = jax.ShapeDtypeStruct((items, width), f32)

    stage = pltpu.VMEM((LANES, width), f32)
    scales = scales_of(embeddings, feature_parts)
    block = min(items, BLOCK)
    steps = (items // block,)
    local = pltpu.CompilerParams(vmem_limit_bytes=VMEM_BYTES)
    by_rows = pl.BlockSpec((block, width), lambda at: (at, 0))
    by_columns = pl.BlockSpec((width, block), lambda at: (0, at))
    table = pl.BlockSpec((total, width), lambda at: (0, 0))
    own = pl.BlockSpec(first_old.shape, lambda at: (0, 0))
    own_shape = jax.ShapeDtypeStruct(first_old.shape, f32)
    normed, first_sums = pl.pallas_call(
        first_kernel,
        out_shape=(row_items, row_sums),
        grid=steps,
        in_specs=[SMEM, by_columns, pl.BlockSpec((1, block), lambda at: (0, at))],
        out_specs=(by_rows, table),
        scratch_shapes=[stage, stage] + piles,
        compiler_params=local,
        cost_estimate=cost,
        name="first_sums",
    )(first_codes, embeddings, scales)
    first_whole, first_own, inverse = exchange(first_sums, first_old, owners, 1, codes=(first_codes, second_codes))
    middle, second_sums, first_new = pl.pallas_call(
        second_kernel,
        out_shape=(row_items, row_sums, own_shape),
        grid=steps,
        in_specs=[SMEM, SMEM, by_rows, table, own],
        out_specs=(by_rows, table, own),
        scratch_shapes=piles,
        compiler_params=local,
        cost_estimate=cost,
        name="second_sums",
    )(first_codes, second_codes, normed, first_whole, first_own)
    second_whole, second_own = exchange(second_sums, second_old, owners, 2, inverse=inverse)
    leftover, second_new = pl.pallas_call(
        last_kernel,
        out_shape=(jax.ShapeDtypeStruct((width, items), f32), own_shape),
        grid=steps,
        in_specs=[SMEM, by_rows, table, own],
        out_specs=(by_columns, own),
        scratch_shapes=[stage, stage],
        compiler_params=local,
        cost_estimate=cost,
        name="leftover",
    )(second_codes, middle, second_whole, second_own)
    return (first_new, second_new, leftover)


def solution(mesh):
    in_specs = (P("code", "item"), P("item"), P("item"), P("code", "item"), P("code", "item"))
    out_specs = (P("code", "item"), P("code", "item"), P("code", "item"))
    return jax.shard_map(
        functools.partial(on_device, mesh.shape["item"], mesh.shape["code"]),
        mesh=mesh,
        in_specs=in_specs,
        out_specs=out_specs,
        check_vma=False,
    )
```

```python
import functools
import itertools

import jax
import jax.numpy as jnp
from jax import lax
from jax.experimental import pallas as pl
from jax.experimental.pallas import tpu as pltpu
from jax.sharding import PartitionSpec as P

D = 512
LANES = 128
FIRST_PILES = 4
FIRST_GROUP = 16
SECOND_PILES = 8
SECOND_GROUP = 32
GROUP = 16
SPAN = 128
BLOCK = 2048
PATHS = 4
MIB = 2**20
VMEM_BYTES = 56 * MIB

VMEM = pl.BlockSpec(memory_space=pltpu.VMEM)
SMEM = pl.BlockSpec(memory_space=pltpu.SMEM)
ANY = pl.BlockSpec(memory_space=pl.ANY)


def flip(me, bits):
    other = me
    for bit in bits:
        weight = 2**bit
        other = other + weight - 2 * weight * lax.rem(lax.div(me, weight), 2)
    return other


def subsets(bits, choice):
    return [tuple(b for b, c in zip(bits, pick) if c) for pick in itertools.product(choice, repeat=len(bits))]


def scales_kernel(n, e_ref, scale_ref, parts, send_sems, recv_sems):
    me = lax.axis_index("code")
    barrier = pltpu.get_barrier_semaphore()
    for step in range(1, n):
        pl.semaphore_signal(barrier, inc=1, device_id={"code": lax.rem(me + step, n)}, device_id_type=pl.DeviceIdType.MESH)
    items = e_ref.shape[1]
    width = min(items, 8 * LANES)

    @pl.loop(0, items // width)
    def _(at):
        columns = pl.ds(pl.multiple_of(at * width, width), width)
        values = e_ref[:, columns].astype(jnp.float32)
        parts[0, :, columns] = jnp.sum(values * values, axis=0, keepdims=True)

    pl.semaphore_wait(barrier, n - 1)
    copies = []
    for step in range(1, n):
        copy = pltpu.make_async_remote_copy(
            src_ref=parts.at[0],
            dst_ref=parts.at[step],
            send_sem=send_sems.at[step],
            recv_sem=recv_sems.at[step],
            device_id={"code": lax.rem(me + step, n)},
            device_id_type=pl.DeviceIdType.MESH,
        )
        copy.start()
        copies.append(copy)
    for copy in copies:
        copy.wait()
    squares = parts[0]
    for step in range(1, n):
        squares = squares + parts[step]
    scale_ref[...] = lax.rsqrt(squares / D + 1e-06)


def scales_of(embeddings, n):
    items = embeddings.shape[1]
    return pl.pallas_call(
        functools.partial(scales_kernel, n),
        out_shape=jax.ShapeDtypeStruct((1, items), jnp.float32),
        in_specs=[VMEM],
        out_specs=VMEM,
        scratch_shapes=[
            pltpu.VMEM((n, 1, items), jnp.float32),
            pltpu.SemaphoreType.DMA((n,)),
            pltpu.SemaphoreType.DMA((n,)),
        ],
        compiler_params=pltpu.CompilerParams(collective_id=0, has_side_effects=True, vmem_limit_bytes=VMEM_BYTES),
        cost_estimate=pl.CostEstimate(flops=0, bytes_accessed=16 * MIB, transcendentals=0),
        name="scales",
    )(embeddings)


def count_codes(codes_ref, total):
    items = codes_ref.shape[1]
    width = min(items, 8 * LANES)
    high_of = lax.broadcasted_iota(jnp.int32, (total // LANES, width), 0)
    low_of = lax.broadcasted_iota(jnp.int32, (LANES, width), 0)

    def add(at, held):
        codes = codes_ref[:, pl.ds(pl.multiple_of(at * width, width), width)]
        high = jnp.where(lax.shift_right_logical(codes, 7) == high_of, 1.0, 0.0).astype(jnp.bfloat16)
        low = jnp.where(lax.bitwise_and(codes, LANES - 1) == low_of, 1.0, 0.0).astype(jnp.bfloat16)
        return held + lax.dot_general(high, low, (((1,), (1,)), ((), ())), preferred_element_type=jnp.float32)

    return lax.fori_loop(0, items // width, add, jnp.zeros((total // LANES, LANES), jnp.float32))


def clear(piles):
    rows = piles[0].shape[0]
    step = min(rows, 128)

    @pl.loop(0, rows // step)
    def _(at):
        for pile in piles:
            pile[pl.ds(pl.multiple_of(at * step, step), step), :] = jnp.zeros((step, pile.shape[1]), pile.dtype)


def merge(piles):
    rows = piles[0].shape[0]
    step = min(rows, 128)

    @pl.loop(0, rows // step)
    def _(at):
        where = pl.ds(pl.multiple_of(at * step, step), step)
        parts = [pile[where, :] for pile in piles]
        while len(parts) > 1:
            parts = [a + b for a, b in zip(parts[::2], parts[1::2])]
        piles[0][where, :] = parts[0]


def add_rows(piles, codes, rows):
    held = [piles[at % len(piles)][pl.ds(code, 1), :] for at, code in enumerate(codes)]
    results = []
    for at, code in enumerate(codes):
        value = held[at]
        for earlier in range(at % len(piles), at, len(piles)):
            value = jnp.where(code == codes[earlier], results[earlier], value)
        results.append(value + rows[at])
    for at, code in enumerate(codes):
        piles[at % len(piles)][pl.ds(code, 1), :] = results[at]


def first_kernel(codes_ref, e_ref, scale_ref, normed_ref, sums_ref, left, right, *more):
    piles = (sums_ref,) + more
    items = e_ref.shape[1]
    offset = pl.program_id(0) * items

    @pl.when(pl.program_id(0) == 0)
    def _():
        clear(piles)

    @pl.loop(0, items // (2 * LANES))
    def _(at):
        base = pl.multiple_of(at * 2 * LANES, 2 * LANES)
        for which, stage in enumerate((left, right)):
            span = pl.ds(pl.multiple_of(base + which * LANES, LANES), LANES)
            block = (e_ref[:, span].astype(jnp.float32) * scale_ref[:, span]).T
            stage[...] = block
            normed_ref[span, :] = block
        for which, stage in enumerate((left, right)):
            for start in range(0, LANES, FIRST_GROUP):
                rows = [stage[start + j:start + j + 1, :] for j in range(FIRST_GROUP)]
                add_rows(piles, [codes_ref[offset + base + which * LANES + start + j] for j in range(FIRST_GROUP)], rows)

    @pl.when(pl.program_id(0) == pl.num_programs(0) - 1)
    def _():
        merge(piles)


def second_kernel(first_ref, second_ref, normed_ref, table_ref, own_ref, middle_ref, sums_ref, new_ref, *more):
    piles = (sums_ref,) + more
    items = normed_ref.shape[0]
    offset = pl.program_id(0) * items

    @pl.when(pl.program_id(0) == 0)
    def _():
        new_ref[...] = own_ref[...]
        clear(piles)

    @pl.loop(0, items // SPAN)
    def _(at):
        for start in range(0, SPAN, SECOND_GROUP):
            base = pl.multiple_of(at * SPAN + start, SECOND_GROUP)
            rows = [
                normed_ref[pl.ds(base + j, 1), :] - table_ref[pl.ds(first_ref[offset + base + j], 1), :]
                for j in range(SECOND_GROUP)
            ]
            add_rows(piles, [second_ref[offset + base + j] for j in range(SECOND_GROUP)], rows)
            for j in range(SECOND_GROUP):
                middle_ref[pl.ds(base + j, 1), :] = rows[j]

    @pl.when(pl.program_id(0) == pl.num_programs(0) - 1)
    def _():
        merge(piles)


def last_kernel(codes_ref, middle_ref, table_ref, own_ref, out_ref, new_ref, left, right):
    block = middle_ref.shape[0]
    start = pl.program_id(0) * block

    @pl.when(pl.program_id(0) == 0)
    def _():
        new_ref[...] = own_ref[...]

    @pl.loop(0, block // (2 * LANES))
    def _(at):
        base = pl.multiple_of(at * 2 * LANES, 2 * LANES)
        for which, stage in enumerate((left, right)):
            for group in range(0, LANES, GROUP):
                rows = [
                    table_ref[pl.ds(codes_ref[start + base + which * LANES + group + j], 1), :] for j in range(GROUP)
                ]
                for j in range(GROUP):
                    stage[group + j:group + j + 1, :] = rows[j]
        for which, stage in enumerate((left, right)):
            span = pl.ds(pl.multiple_of(base + which * LANES, LANES), LANES)
            out_ref[:, span] = (middle_ref[span, :] - stage[...]).T


def exchange_kernel(n, counting, sums_ref, old_ref, *refs):
    if counting:
        *codes_refs, whole_ref, own_ref, inverse_ref = refs[:5]
        counts, got, send_counts, recv_counts = refs[-4:]
        refs = refs[5:-4]
    else:
        inverse_ref, whole_ref, own_ref = refs[:3]
        refs = refs[3:]
    old, inverse, fresh, kept, slots, keep_sems, own_sems, send_in, recv_in, send_out, recv_out = refs
    levels = n.bit_length() - 1
    me = lax.axis_index("item")
    size = sums_ref.shape[0] // n
    part = size // PATHS
    rest = list(range(1, levels))
    orders = [[0] + (rest if path % 2 == 0 else rest[::-1]) for path in range(PATHS)]

    def block(owner, path):
        return pl.ds(pl.multiple_of(owner * size + path * part, part), part)

    place_in, place_out = {}, {}
    for path, order in enumerate(orders):
        for step in range(levels):
            for far in subsets(order[step + 1:], (1, 0)):
                place_in[path, step, frozenset(far)] = len(place_in)
            for held in subsets(order[::-1][:step], (0, 1)):
                place_out[path, step, frozenset(held)] = len(place_out)
    place_kept = {
        (path, frozenset(far)): at
        for at, (path, far) in enumerate(
            (path, far) for path in range(PATHS) for far in subsets(orders[path][1:], (1, 0))
        )
    }
    sent = []

    def sum_copy(path, step, far, source):
        slot = place_in[path, step, frozenset(far)]
        return pltpu.make_async_remote_copy(
            src_ref=source,
            dst_ref=slots.at[slot],
            send_sem=send_in.at[slot],
            recv_sem=recv_in.at[slot],
            device_id={"item": flip(me, [orders[path][step]])},
            device_id_type=pl.DeviceIdType.MESH,
        )

    def new_copy(path, step, held, source, rows):
        slot = place_out[path, step, frozenset(held)]
        return pltpu.make_async_remote_copy(
            src_ref=source,
            dst_ref=whole_ref.at[rows],
            send_sem=send_out.at[slot],
            recv_sem=recv_out.at[slot],
            device_id={"item": flip(me, [orders[path][::-1][step]])},
            device_id_type=pl.DeviceIdType.MESH,
        )

    def send(copy):
        copy.start()
        sent.append(copy)

    def keep_copy(path, far):
        slot = place_kept[path, frozenset(far)]
        return pltpu.make_async_copy(sums_ref.at[block(flip(me, far), path)], kept.at[slot], keep_sems.at[slot])

    def fars_of(step):
        return list(zip(*(subsets(order[step + 1:], (1, 0)) for order in orders)))

    def open_with(fars):
        for path, far in enumerate(fars):
            send(sum_copy(path, 0, far, sums_ref.at[block(flip(me, (0,) + far), path)]))

    def count_copy(step):
        there = lax.rem(me + step, n)
        return pltpu.make_async_remote_copy(
            src_ref=counts.at[there],
            dst_ref=got.at[step],
            send_sem=send_counts.at[step],
            recv_sem=recv_counts.at[step],
            device_id={"item": there},
            device_id_type=pl.DeviceIdType.MESH,
        )

    def spread(level_inverse):
        for at in range(size // LANES):
            span = slice(at * LANES, (at + 1) * LANES)
            inverse[span, :] = jnp.broadcast_to(level_inverse[at:at + 1, :], (old.shape[1], LANES)).T

    barrier = pltpu.get_barrier_semaphore()
    if counting:
        peers = [lax.rem(me + step, n) for step in range(1, n)]
    else:
        peers = [flip(me, [bit]) for bit in range(levels)]
    for peer in peers:
        pl.semaphore_signal(barrier, inc=1, device_id={"item": peer}, device_id_type=pl.DeviceIdType.MESH)
    for fars in fars_of(0):
        for path, far in enumerate(fars):
            keep_copy(path, far).start()
    pl.semaphore_wait(barrier, len(peers))

    opening = fars_of(0)
    middle = len(opening) // 2
    for fars in opening[:middle]:
        open_with(fars)
    for step in range(levels):
        for at, fars in enumerate(fars_of(step)):
            if step == 0 and at == middle:
                for later in opening[middle:]:
                    open_with(later)
            for path, far in enumerate(fars):
                slot = place_in[path, step, frozenset(far)]
                sum_copy(path, step, far, slots.at[slot]).wait_recv()
                if step == 0:
                    keep_copy(path, far).wait()
                    mine = kept[place_kept[path, frozenset(far)]]
                else:
                    mine = slots[place_in[path, step - 1, frozenset(far)]]
                total = slots[slot] + mine
                if step < levels - 1:
                    slots[slot] = total
                    ahead = orders[path][step + 1]
                    if ahead in far:
                        send(sum_copy(path, step + 1, tuple(b for b in far if b != ahead), slots.at[slot]))
                else:
                    rows = pl.ds(path * part, part)
                    fresh[rows, :] = old[rows, :] + total * inverse[rows, :]
                    send(new_copy(path, 0, (), fresh.at[rows], block(me, path)))
                    pltpu.make_async_copy(fresh.at[rows], whole_ref.at[block(me, path)], own_sems.at[path]).start()
        if step == 0:
            for at in range(size // LANES):
                span = slice(at * LANES, (at + 1) * LANES)
                old[span, :] = (0.5 * old_ref[:, span]).T
            if counting:
                rows = counts.shape[2]
                for level, codes_ref in enumerate(codes_refs):
                    held = count_codes(codes_ref, n * size)
                    for owner in range(n):
                        counts[owner, level] = held[owner * rows:(owner + 1) * rows]
                for away in range(1, n):
                    send(count_copy(away))
            else:
                spread(inverse_ref[...])
        if step == levels - 2 and counting:
            held = counts[me]
            for away in range(1, n):
                count_copy(away).wait_recv()
                held = held + got[away]
            both = 0.5 / (held + 1.0)
            spread(both[0])
            inverse_ref[...] = both[1]
    for later in range(1, levels):
        for path in range(PATHS):
            send(new_copy(path, later, (), fresh.at[pl.ds(path * part, part)], block(me, path)))

    for step in range(levels):
        for helds in zip(*(subsets(order[::-1][:step], (0, 1)) for order in orders)):
            for path, held in enumerate(helds):
                got = held + (orders[path][::-1][step],)
                rows = block(flip(me, got), path)
                new_copy(path, step, held, whole_ref.at[rows], rows).wait_recv()
                for later in range(step + 1, levels):
                    send(new_copy(path, later, got, whole_ref.at[rows], rows))
        if step == 0:
            for at in range(size // LANES):
                span = slice(at * LANES, (at + 1) * LANES)
                own_ref[:, span] = fresh[span, :].T
    for path in range(PATHS):
        pltpu.make_async_copy(
            fresh.at[pl.ds(path * part, part)], whole_ref.at[block(me, path)], own_sems.at[path]
        ).wait()
    for copy in sent:
        copy.wait_send()


def exchange(sums, old, n, collective_id, inverse=None, codes=()):
    rows, width = sums.shape
    size = rows // n
    part = size // PATHS
    count = PATHS * (n - 1)
    out_shape = [jax.ShapeDtypeStruct(sums.shape, jnp.float32), jax.ShapeDtypeStruct((width, size), jnp.float32)]
    scratch = [
        pltpu.VMEM((size, width), jnp.float32),
        pltpu.VMEM((size, width), jnp.float32),
        pltpu.VMEM((size, width), jnp.float32),
        pltpu.VMEM((PATHS * n // 2, part, width), jnp.float32),
        pltpu.VMEM((count, part, width), jnp.float32),
        pltpu.SemaphoreType.DMA((PATHS * n // 2,)),
        pltpu.SemaphoreType.DMA((PATHS,)),
        pltpu.SemaphoreType.DMA((count,)),
        pltpu.SemaphoreType.DMA((count,)),
        pltpu.SemaphoreType.DMA((count,)),
        pltpu.SemaphoreType.DMA((count,)),
    ]
    if codes:
        inputs = (sums, old) + tuple(level[None, :] for level in codes)
        out_shape.append(jax.ShapeDtypeStruct((size // LANES, LANES), jnp.float32))
        scratch += [pltpu.VMEM((n, len(codes), size // LANES, LANES), jnp.float32)] * 2
        scratch += [pltpu.SemaphoreType.DMA((n,))] * 2
    else:
        inputs = (sums, old, inverse)
    return pl.pallas_call(
        functools.partial(exchange_kernel, n, bool(codes)),
        out_shape=out_shape,
        in_specs=[ANY] + [VMEM] * (len(inputs) - 1),
        out_specs=[ANY] + [VMEM] * (len(out_shape) - 1),
        scratch_shapes=scratch,
        compiler_params=pltpu.CompilerParams(
            collective_id=collective_id, has_side_effects=True, vmem_limit_bytes=VMEM_BYTES
        ),
        cost_estimate=pl.CostEstimate(flops=0, bytes_accessed=128 * MIB, transcendentals=0),
        name="exchange",
    )(*inputs)


def on_device(owners, feature_parts, embeddings, first_codes, second_codes, first_old, second_old):
    width, items = embeddings.shape
    total = first_old.shape[1] * owners
    f32 = jnp.float32
    cost = pl.CostEstimate(flops=0, bytes_accessed=64 * MIB, transcendentals=0)
    pile = pltpu.VMEM((total, width), f32)
    row_sums = jax.ShapeDtypeStruct((total, width), f32)
    row_items = jax.ShapeDtypeStruct((items, width), f32)

    stage = pltpu.VMEM((LANES, width), f32)
    scales = scales_of(embeddings, feature_parts)
    block = min(items, BLOCK)
    steps = (items // block,)
    local = pltpu.CompilerParams(vmem_limit_bytes=VMEM_BYTES)
    by_rows = pl.BlockSpec((block, width), lambda at: (at, 0))
    by_columns = pl.BlockSpec((width, block), lambda at: (0, at))
    table = pl.BlockSpec((total, width), lambda at: (0, 0))
    own = pl.BlockSpec(first_old.shape, lambda at: (0, 0))
    own_shape = jax.ShapeDtypeStruct(first_old.shape, f32)
    normed, first_sums = pl.pallas_call(
        first_kernel,
        out_shape=(row_items, row_sums),
        grid=steps,
        in_specs=[SMEM, by_columns, pl.BlockSpec((1, block), lambda at: (0, at))],
        out_specs=(by_rows, table),
        scratch_shapes=[stage, stage] + [pile] * (FIRST_PILES - 1),
        compiler_params=local,
        cost_estimate=cost,
        name="first_sums",
    )(first_codes, embeddings, scales)
    first_whole, first_own, inverse = exchange(first_sums, first_old, owners, 1, codes=(first_codes, second_codes))
    middle, second_sums, first_new = pl.pallas_call(
        second_kernel,
        out_shape=(row_items, row_sums, own_shape),
        grid=steps,
        in_specs=[SMEM, SMEM, by_rows, table, own],
        out_specs=(by_rows, table, own),
        scratch_shapes=[pile] * (SECOND_PILES - 1),
        compiler_params=local,
        cost_estimate=cost,
        name="second_sums",
    )(first_codes, second_codes, normed, first_whole, first_own)
    second_whole, second_own = exchange(second_sums, second_old, owners, 2, inverse=inverse)
    leftover, second_new = pl.pallas_call(
        last_kernel,
        out_shape=(jax.ShapeDtypeStruct((width, items), f32), own_shape),
        grid=steps,
        in_specs=[SMEM, by_rows, table, own],
        out_specs=(by_columns, own),
        scratch_shapes=[stage, stage],
        compiler_params=local,
        cost_estimate=cost,
        name="leftover",
    )(second_codes, middle, second_whole, second_own)
    return (first_new, second_new, leftover)


def solution(mesh):
    in_specs = (P("code", "item"), P("item"), P("item"), P("code", "item"), P("code", "item"))
    out_specs = (P("code", "item"), P("code", "item"), P("code", "item"))
    return jax.shard_map(
        functools.partial(on_device, mesh.shape["item"], mesh.shape["code"]),
        mesh=mesh,
        in_specs=in_specs,
        out_specs=out_specs,
        check_vma=False,
    )
```

```python
import functools
import itertools

import jax
import jax.numpy as jnp
from jax import lax
from jax.experimental import pallas as pl
from jax.experimental.pallas import tpu as pltpu
from jax.sharding import PartitionSpec as P

D = 512
LANES = 128
PILES = 8
GROUP = PILES
SPAN = 128
BLOCK = 1024
PATHS = 4
MIB = 2**20
VMEM_BYTES = 56 * MIB

VMEM = pl.BlockSpec(memory_space=pltpu.VMEM)
SMEM = pl.BlockSpec(memory_space=pltpu.SMEM)
ANY = pl.BlockSpec(memory_space=pl.ANY)


def flip(me, bits):
    other = me
    for bit in bits:
        weight = 2**bit
        other = other + weight - 2 * weight * lax.rem(lax.div(me, weight), 2)
    return other


def subsets(bits, choice):
    return [tuple(b for b, c in zip(bits, pick) if c) for pick in itertools.product(choice, repeat=len(bits))]


def scales_kernel(n, e_ref, scale_ref, parts, send_sems, recv_sems):
    me = lax.axis_index("code")
    barrier = pltpu.get_barrier_semaphore()
    for step in range(1, n):
        pl.semaphore_signal(barrier, inc=1, device_id={"code": lax.rem(me + step, n)}, device_id_type=pl.DeviceIdType.MESH)
    items = e_ref.shape[1]
    width = min(items, 8 * LANES)

    @pl.loop(0, items // width)
    def _(at):
        columns = pl.ds(pl.multiple_of(at * width, width), width)
        values = e_ref[:, columns].astype(jnp.float32)
        parts[0, :, columns] = jnp.sum(values * values, axis=0, keepdims=True)

    pl.semaphore_wait(barrier, n - 1)
    copies = []
    for step in range(1, n):
        copy = pltpu.make_async_remote_copy(
            src_ref=parts.at[0],
            dst_ref=parts.at[step],
            send_sem=send_sems.at[step],
            recv_sem=recv_sems.at[step],
            device_id={"code": lax.rem(me + step, n)},
            device_id_type=pl.DeviceIdType.MESH,
        )
        copy.start()
        copies.append(copy)
    for copy in copies:
        copy.wait()
    squares = parts[0]
    for step in range(1, n):
        squares = squares + parts[step]
    scale_ref[...] = lax.rsqrt(squares / D + 1e-06)


def scales_of(embeddings, n):
    items = embeddings.shape[1]
    return pl.pallas_call(
        functools.partial(scales_kernel, n),
        out_shape=jax.ShapeDtypeStruct((1, items), jnp.float32),
        in_specs=[VMEM],
        out_specs=VMEM,
        scratch_shapes=[
            pltpu.VMEM((n, 1, items), jnp.float32),
            pltpu.SemaphoreType.DMA((n,)),
            pltpu.SemaphoreType.DMA((n,)),
        ],
        compiler_params=pltpu.CompilerParams(collective_id=0, has_side_effects=True, vmem_limit_bytes=VMEM_BYTES),
        cost_estimate=pl.CostEstimate(flops=0, bytes_accessed=16 * MIB, transcendentals=0),
        name="scales",
    )(embeddings)


def count_codes(codes_ref, total):
    items = codes_ref.shape[1]
    width = min(items, 8 * LANES)
    high_of = lax.broadcasted_iota(jnp.int32, (total // LANES, width), 0)
    low_of = lax.broadcasted_iota(jnp.int32, (LANES, width), 0)

    def add(at, held):
        codes = codes_ref[:, pl.ds(pl.multiple_of(at * width, width), width)]
        high = jnp.where(lax.shift_right_logical(codes, 7) == high_of, 1.0, 0.0).astype(jnp.bfloat16)
        low = jnp.where(lax.bitwise_and(codes, LANES - 1) == low_of, 1.0, 0.0).astype(jnp.bfloat16)
        return held + lax.dot_general(high, low, (((1,), (1,)), ((), ())), preferred_element_type=jnp.float32)

    return lax.fori_loop(0, items // width, add, jnp.zeros((total // LANES, LANES), jnp.float32))


def clear(piles):
    rows = piles[0].shape[0]
    step = min(rows, 128)

    @pl.loop(0, rows // step)
    def _(at):
        for pile in piles:
            pile[pl.ds(pl.multiple_of(at * step, step), step), :] = jnp.zeros((step, pile.shape[1]), pile.dtype)


def merge(piles):
    rows = piles[0].shape[0]
    step = min(rows, 128)

    @pl.loop(0, rows // step)
    def _(at):
        where = pl.ds(pl.multiple_of(at * step, step), step)
        parts = [pile[where, :] for pile in piles]
        while len(parts) > 1:
            parts = [a + b for a, b in zip(parts[::2], parts[1::2])]
        piles[0][where, :] = parts[0]


def add_rows(piles, codes, rows):
    held = [pile[pl.ds(code, 1), :] for pile, code in zip(piles, codes)]
    results = [value + row for value, row in zip(held, rows)]
    for pile, code, result in zip(piles, codes, results):
        pile[pl.ds(code, 1), :] = result


def first_kernel(codes_ref, e_ref, scale_ref, normed_ref, sums_ref, left, right, *more):
    piles = (sums_ref,) + more
    items = e_ref.shape[1]
    offset = pl.program_id(0) * items

    @pl.when(pl.program_id(0) == 0)
    def _():
        clear(piles)

    @pl.loop(0, items // (2 * LANES))
    def _(at):
        base = pl.multiple_of(at * 2 * LANES, 2 * LANES)
        for which, stage in enumerate((left, right)):
            span = pl.ds(pl.multiple_of(base + which * LANES, LANES), LANES)
            block = (e_ref[:, span].astype(jnp.float32) * scale_ref[:, span]).T
            stage[...] = block
            normed_ref[span, :] = block
        for which, stage in enumerate((left, right)):
            for start in range(0, LANES, GROUP):
                rows = [stage[start + j:start + j + 1, :] for j in range(GROUP)]
                add_rows(piles, [codes_ref[offset + base + which * LANES + start + j] for j in range(GROUP)], rows)

    @pl.when(pl.program_id(0) == pl.num_programs(0) - 1)
    def _():
        merge(piles)


def second_kernel(first_ref, second_ref, normed_ref, table_ref, own_ref, middle_ref, sums_ref, new_ref, *more):
    piles = (sums_ref,) + more
    items = normed_ref.shape[0]
    offset = pl.program_id(0) * items

    @pl.when(pl.program_id(0) == 0)
    def _():
        new_ref[...] = own_ref[...]
        clear(piles)

    @pl.loop(0, items // SPAN)
    def _(at):
        for start in range(0, SPAN, GROUP):
            base = pl.multiple_of(at * SPAN + start, GROUP)
            rows = [
                normed_ref[pl.ds(base + j, 1), :] - table_ref[pl.ds(first_ref[offset + base + j], 1), :]
                for j in range(GROUP)
            ]
            add_rows(piles, [second_ref[offset + base + j] for j in range(GROUP)], rows)
            for j in range(GROUP):
                middle_ref[pl.ds(base + j, 1), :] = rows[j]

    @pl.when(pl.program_id(0) == pl.num_programs(0) - 1)
    def _():
        merge(piles)


def last_kernel(codes_ref, middle_ref, table_ref, own_ref, out_ref, new_ref, left, right):
    block = middle_ref.shape[0]
    start = pl.program_id(0) * block

    @pl.when(pl.program_id(0) == 0)
    def _():
        new_ref[...] = own_ref[...]

    @pl.loop(0, block // (2 * LANES))
    def _(at):
        base = pl.multiple_of(at * 2 * LANES, 2 * LANES)
        for which, stage in enumerate((left, right)):
            for group in range(0, LANES, GROUP):
                rows = [
                    table_ref[pl.ds(codes_ref[start + base + which * LANES + group + j], 1), :] for j in range(GROUP)
                ]
                for j in range(GROUP):
                    stage[group + j:group + j + 1, :] = rows[j]
        for which, stage in enumerate((left, right)):
            span = pl.ds(pl.multiple_of(base + which * LANES, LANES), LANES)
            out_ref[:, span] = (middle_ref[span, :] - stage[...]).T


def exchange_kernel(n, counting, sums_ref, old_ref, *refs):
    if counting:
        *codes_refs, whole_ref, own_ref, inverse_ref = refs[:5]
        counts, got, send_counts, recv_counts = refs[-4:]
        refs = refs[5:-4]
    else:
        inverse_ref, whole_ref, own_ref = refs[:3]
        refs = refs[3:]
    old, inverse, fresh, kept, slots, keep_sems, own_sems, send_in, recv_in, send_out, recv_out = refs
    levels = n.bit_length() - 1
    me = lax.axis_index("item")
    size = sums_ref.shape[0] // n
    part = size // PATHS
    rest = list(range(1, levels))
    orders = [[0] + (rest if path % 2 == 0 else rest[::-1]) for path in range(PATHS)]

    def block(owner, path):
        return pl.ds(pl.multiple_of(owner * size + path * part, part), part)

    place_in, place_out = {}, {}
    for path, order in enumerate(orders):
        for step in range(levels):
            for far in subsets(order[step + 1:], (1, 0)):
                place_in[path, step, frozenset(far)] = len(place_in)
            for held in subsets(order[::-1][:step], (0, 1)):
                place_out[path, step, frozenset(held)] = len(place_out)
    place_kept = {
        (path, frozenset(far)): at
        for at, (path, far) in enumerate(
            (path, far) for path in range(PATHS) for far in subsets(orders[path][1:], (1, 0))
        )
    }
    sent = []

    def sum_copy(path, step, far, source):
        slot = place_in[path, step, frozenset(far)]
        return pltpu.make_async_remote_copy(
            src_ref=source,
            dst_ref=slots.at[slot],
            send_sem=send_in.at[slot],
            recv_sem=recv_in.at[slot],
            device_id={"item": flip(me, [orders[path][step]])},
            device_id_type=pl.DeviceIdType.MESH,
        )

    def new_copy(path, step, held, source, rows):
        slot = place_out[path, step, frozenset(held)]
        return pltpu.make_async_remote_copy(
            src_ref=source,
            dst_ref=whole_ref.at[rows],
            send_sem=send_out.at[slot],
            recv_sem=recv_out.at[slot],
            device_id={"item": flip(me, [orders[path][::-1][step]])},
            device_id_type=pl.DeviceIdType.MESH,
        )

    def send(copy):
        copy.start()
        sent.append(copy)

    def keep_copy(path, far):
        slot = place_kept[path, frozenset(far)]
        return pltpu.make_async_copy(sums_ref.at[block(flip(me, far), path)], kept.at[slot], keep_sems.at[slot])

    def fars_of(step):
        return list(zip(*(subsets(order[step + 1:], (1, 0)) for order in orders)))

    def open_with(fars):
        for path, far in enumerate(fars):
            send(sum_copy(path, 0, far, sums_ref.at[block(flip(me, (0,) + far), path)]))

    def count_copy(step):
        there = lax.rem(me + step, n)
        return pltpu.make_async_remote_copy(
            src_ref=counts.at[there],
            dst_ref=got.at[step],
            send_sem=send_counts.at[step],
            recv_sem=recv_counts.at[step],
            device_id={"item": there},
            device_id_type=pl.DeviceIdType.MESH,
        )

    def spread(level_inverse):
        for at in range(size // LANES):
            span = slice(at * LANES, (at + 1) * LANES)
            inverse[span, :] = jnp.broadcast_to(level_inverse[at:at + 1, :], (old.shape[1], LANES)).T

    barrier = pltpu.get_barrier_semaphore()
    if counting:
        peers = [lax.rem(me + step, n) for step in range(1, n)]
    else:
        peers = [flip(me, [bit]) for bit in range(levels)]
    for peer in peers:
        pl.semaphore_signal(barrier, inc=1, device_id={"item": peer}, device_id_type=pl.DeviceIdType.MESH)
    for fars in fars_of(0):
        for path, far in enumerate(fars):
            keep_copy(path, far).start()
    pl.semaphore_wait(barrier, len(peers))

    opening = fars_of(0)
    middle = len(opening) // 2
    for fars in opening[:middle]:
        open_with(fars)
    for step in range(levels):
        for at, fars in enumerate(fars_of(step)):
            if step == 0 and at == middle:
                for later in opening[middle:]:
                    open_with(later)
            for path, far in enumerate(fars):
                slot = place_in[path, step, frozenset(far)]
                sum_copy(path, step, far, slots.at[slot]).wait_recv()
                if step == 0:
                    keep_copy(path, far).wait()
                    mine = kept[place_kept[path, frozenset(far)]]
                else:
                    mine = slots[place_in[path, step - 1, frozenset(far)]]
                total = slots[slot] + mine
                if step < levels - 1:
                    slots[slot] = total
                    ahead = orders[path][step + 1]
                    if ahead in far:
                        send(sum_copy(path, step + 1, tuple(b for b in far if b != ahead), slots.at[slot]))
                else:
                    rows = pl.ds(path * part, part)
                    fresh[rows, :] = old[rows, :] + total * inverse[rows, :]
                    send(new_copy(path, 0, (), fresh.at[rows], block(me, path)))
                    pltpu.make_async_copy(fresh.at[rows], whole_ref.at[block(me, path)], own_sems.at[path]).start()
        if step == 0:
            for at in range(size // LANES):
                span = slice(at * LANES, (at + 1) * LANES)
                old[span, :] = (0.5 * old_ref[:, span]).T
            if counting:
                rows = counts.shape[2]
                for level, codes_ref in enumerate(codes_refs):
                    held = count_codes(codes_ref, n * size)
                    for owner in range(n):
                        counts[owner, level] = held[owner * rows:(owner + 1) * rows]
                for away in range(1, n):
                    send(count_copy(away))
            else:
                spread(inverse_ref[...])
        if step == levels - 2 and counting:
            held = counts[me]
            for away in range(1, n):
                count_copy(away).wait_recv()
                held = held + got[away]
            both = 0.5 / (held + 1.0)
            spread(both[0])
            inverse_ref[...] = both[1]
    for later in range(1, levels):
        for path in range(PATHS):
            send(new_copy(path, later, (), fresh.at[pl.ds(path * part, part)], block(me, path)))

    for step in range(levels):
        for helds in zip(*(subsets(order[::-1][:step], (0, 1)) for order in orders)):
            for path, held in enumerate(helds):
                got = held + (orders[path][::-1][step],)
                rows = block(flip(me, got), path)
                new_copy(path, step, held, whole_ref.at[rows], rows).wait_recv()
                for later in range(step + 1, levels):
                    send(new_copy(path, later, got, whole_ref.at[rows], rows))
        if step == 0:
            for at in range(size // LANES):
                span = slice(at * LANES, (at + 1) * LANES)
                own_ref[:, span] = fresh[span, :].T
    for path in range(PATHS):
        pltpu.make_async_copy(
            fresh.at[pl.ds(path * part, part)], whole_ref.at[block(me, path)], own_sems.at[path]
        ).wait()
    for copy in sent:
        copy.wait_send()


def exchange(sums, old, n, collective_id, inverse=None, codes=()):
    rows, width = sums.shape
    size = rows // n
    part = size // PATHS
    count = PATHS * (n - 1)
    out_shape = [jax.ShapeDtypeStruct(sums.shape, jnp.float32), jax.ShapeDtypeStruct((width, size), jnp.float32)]
    scratch = [
        pltpu.VMEM((size, width), jnp.float32),
        pltpu.VMEM((size, width), jnp.float32),
        pltpu.VMEM((size, width), jnp.float32),
        pltpu.VMEM((PATHS * n // 2, part, width), jnp.float32),
        pltpu.VMEM((count, part, width), jnp.float32),
        pltpu.SemaphoreType.DMA((PATHS * n // 2,)),
        pltpu.SemaphoreType.DMA((PATHS,)),
        pltpu.SemaphoreType.DMA((count,)),
        pltpu.SemaphoreType.DMA((count,)),
        pltpu.SemaphoreType.DMA((count,)),
        pltpu.SemaphoreType.DMA((count,)),
    ]
    if codes:
        inputs = (sums, old) + tuple(level[None, :] for level in codes)
        out_shape.append(jax.ShapeDtypeStruct((size // LANES, LANES), jnp.float32))
        scratch += [pltpu.VMEM((n, len(codes), size // LANES, LANES), jnp.float32)] * 2
        scratch += [pltpu.SemaphoreType.DMA((n,))] * 2
    else:
        inputs = (sums, old, inverse)
    return pl.pallas_call(
        functools.partial(exchange_kernel, n, bool(codes)),
        out_shape=out_shape,
        in_specs=[ANY] + [VMEM] * (len(inputs) - 1),
        out_specs=[ANY] + [VMEM] * (len(out_shape) - 1),
        scratch_shapes=scratch,
        compiler_params=pltpu.CompilerParams(
            collective_id=collective_id, has_side_effects=True, vmem_limit_bytes=VMEM_BYTES
        ),
        cost_estimate=pl.CostEstimate(flops=0, bytes_accessed=128 * MIB, transcendentals=0),
        name="exchange",
    )(*inputs)


def on_device(owners, feature_parts, embeddings, first_codes, second_codes, first_old, second_old):
    width, items = embeddings.shape
    total = first_old.shape[1] * owners
    f32 = jnp.float32
    cost = pl.CostEstimate(flops=0, bytes_accessed=64 * MIB, transcendentals=0)
    piles = [pltpu.VMEM((total, width), f32)] * (PILES - 1)
    row_sums = jax.ShapeDtypeStruct((total, width), f32)
    row_items = jax.ShapeDtypeStruct((items, width), f32)

    stage = pltpu.VMEM((LANES, width), f32)
    scales = scales_of(embeddings, feature_parts)
    block = min(items, BLOCK)
    steps = (items // block,)
    local = pltpu.CompilerParams(vmem_limit_bytes=VMEM_BYTES)
    by_rows = pl.BlockSpec((block, width), lambda at: (at, 0))
    by_columns = pl.BlockSpec((width, block), lambda at: (0, at))
    table = pl.BlockSpec((total, width), lambda at: (0, 0))
    own = pl.BlockSpec(first_old.shape, lambda at: (0, 0))
    own_shape = jax.ShapeDtypeStruct(first_old.shape, f32)
    normed, first_sums = pl.pallas_call(
        first_kernel,
        out_shape=(row_items, row_sums),
        grid=steps,
        in_specs=[SMEM, by_columns, pl.BlockSpec((1, block), lambda at: (0, at))],
        out_specs=(by_rows, table),
        scratch_shapes=[stage, stage] + piles,
        compiler_params=local,
        cost_estimate=cost,
        name="first_sums",
    )(first_codes, embeddings, scales)
    first_whole, first_own, inverse = exchange(first_sums, first_old, owners, 1, codes=(first_codes, second_codes))
    middle, second_sums, first_new = pl.pallas_call(
        second_kernel,
        out_shape=(row_items, row_sums, own_shape),
        grid=steps,
        in_specs=[SMEM, SMEM, by_rows, table, own],
        out_specs=(by_rows, table, own),
        scratch_shapes=piles,
        compiler_params=local,
        cost_estimate=cost,
        name="second_sums",
    )(first_codes, second_codes, normed, first_whole, first_own)
    second_whole, second_own = exchange(second_sums, second_old, owners, 2, inverse=inverse)
    leftover, second_new = pl.pallas_call(
        last_kernel,
        out_shape=(jax.ShapeDtypeStruct((width, items), f32), own_shape),
        grid=steps,
        in_specs=[SMEM, by_rows, table, own],
        out_specs=(by_columns, own),
        scratch_shapes=[stage, stage],
        compiler_params=local,
        cost_estimate=cost,
        name="leftover",
    )(second_codes, middle, second_whole, second_own)
    return (first_new, second_new, leftover)


def solution(mesh):
    in_specs = (P("code", "item"), P("item"), P("item"), P("code", "item"), P("code", "item"))
    out_specs = (P("code", "item"), P("code", "item"), P("code", "item"))
    return jax.shard_map(
        functools.partial(on_device, mesh.shape["item"], mesh.shape["code"]),
        mesh=mesh,
        in_specs=in_specs,
        out_specs=out_specs,
        check_vma=False,
    )
```
